256 devices in a mesh: tg: 4 (over x), tc: 32 (over z, y), sp: 2 (over core).
Axes of the slice: x: 4, y: 4, z: 8, core: 2. Of those that a mesh axis runs over, the one named last changes fastest.
Arguments:
- initial: float32 [512, 128], P('sp'), may hold values from 0.5 to 1.5
- source: float32 [128, 512, 128], P(('tg', 'tc'), 'sp'), may hold values from -0.3 to 0.3
Outputs:
- c_values: float32 [128, 512, 128], P(('tg', 'tc'), 'sp')
- block_mean: float32 [128, 512, 128], P(('tg', 'tc'), 'sp')
The draws below stay inside these ranges and needn't reach their ends.
All inputs are finite; a program needn't handle non-finite values.
Results may differ from the reference program's by a relative error of at most 0.00002.
Values sent between devices are 32-bit elements; how exact they have to be, the bound alone decides.
No kernel may reach another device: no remote copies, remote signals or barrier semaphores. Data moves between devices by JAX's collectives and lax.ppermute only.
A program may use at most 128 MiB of HBM per device.

```python
import jax
import jax.numpy as jnp
from jax import lax

COLS = 128
STEPS = 16
BLOCKS = 128
NROWS = 512


def draw_source(key, part):
    key = jax.random.fold_in(key, 7)
    full_shape = (BLOCKS, NROWS, COLS)
    return jnp.clip(0.05 * jax.random.normal(key, full_shape, jnp.float32), -0.3, 0.3)


def shard_levels(stream_key, shape, pieces, low, top_value):
    def one(dim, parts):
        heights = jax.random.uniform(jax.random.fold_in(jax.random.fold_in(stream_key, 6), dim), (parts,), jnp.float32, low / len(pieces), top_value / len(pieces))
        return jnp.repeat(jnp.exp(heights), shape[dim] // parts).reshape((-1,) + (1,) * (len(shape) - dim - 1))

    factor_of = one(*pieces[0])
    for cut in pieces[1:]:
        factor_of = factor_of * one(*cut)
    return factor_of


def setup_inputs(seed: int = 0) -> dict:
    streams_of = jax.random.split(jax.random.key(seed), 3)
    initial = jnp.clip(0.5 + 1.0 * jax.random.uniform(streams_of[0], (NROWS, COLS), jnp.float32) ** shard_levels(streams_of[0], (NROWS, COLS), ((0, 2),), -0.2, 0.2), 0.5, 1.5)
    source = draw_source(jax.random.fold_in(streams_of[2], 71), 0)
    return dict(initial=initial, source=source)


fine_center = 0.2
fine_behind = 0.25
fine_ahead = 0.15
coarse_center = 0.04
coarse_behind = 0.31
coarse_ahead = 0.17


def stencil(state, center, behind, ahead, row_axis):
    return (center * state + behind * jnp.roll(state, 1, row_axis) + ahead * jnp.roll(state, -1, row_axis)
            + behind * jnp.roll(state, 1, row_axis + 1) + ahead * jnp.roll(state, -1, row_axis + 1))


def advance(state, forcing, step_count):
    def one_step(step_index, current):
        return stencil(current, fine_center, fine_behind, fine_ahead, 1) + forcing
    return lax.fori_loop(0, step_count, one_step, state)


def reference(initial, source):
    first_start = jnp.zeros((BLOCKS, NROWS, COLS), jnp.float32)
    c_guess = advance(first_start, source, STEPS)
    c_start = jnp.concatenate([initial[None], c_guess[:-1]], axis=0)
    defect = advance(c_start, source, STEPS) - c_guess

    def chain(error_now, defect_now):
        error_next = stencil(error_now, coarse_center, coarse_behind, coarse_ahead, 0) + defect_now
        return error_next, error_next

    start_error = jnp.zeros((NROWS, COLS), jnp.float32)
    last_error, errors = lax.scan(chain, start_error, defect)
    c_values = c_guess + errors
    restart = jnp.concatenate([initial[None], c_values[:-1]], axis=0)

    def relax(step_index, carry):
        current, running = carry
        current = stencil(current, fine_center, fine_behind, fine_ahead, 1) + source
        return current, running + current

    final_state, running = lax.fori_loop(0, STEPS - 1, relax, (restart, jnp.zeros_like(restart)))
    block_mean = running / (STEPS - 1)
    return c_values, block_mean
```

```python
import functools

import jax
import jax.numpy as jnp
import numpy as np
from jax import lax
from jax.experimental import pallas as pl
from jax.experimental.pallas import tpu as pltpu
from jax.sharding import PartitionSpec as P

ROWS = 512
HALF = ROWS // 2
COLS = 128
LANES = COLS // 2
BLOCKS = 128
STEPS = 16
DEVICES = 256
AXES = ("tg", "tc", "sp")

fine_center = 0.2
fine_behind = 0.25
fine_ahead = 0.15
coarse_center = 0.04
coarse_behind = 0.31
coarse_ahead = 0.17

HIGHEST = lax.Precision.HIGHEST
N_OPS = 11
TAB_ROWS = 40


def symbol(theta, phi, center, behind, ahead):
    return (
        center
        + behind * np.exp(-1j * theta)
        + ahead * np.exp(1j * theta)
        + behind * np.exp(-1j * phi)
        + ahead * np.exp(1j * phi)
    )


def operators(theta, phi):
    fine = symbol(theta, phi, fine_center, fine_behind, fine_ahead)
    coarse = symbol(theta, phi, coarse_center, coarse_behind, coarse_ahead)
    power, total = np.ones_like(fine), np.zeros_like(fine)
    inner_sum = np.zeros_like(fine)
    inner_power = np.zeros_like(fine)
    for step in range(STEPS):
        total = total + power
        if step < STEPS - 1:
            inner_sum = inner_sum + total
        power = power * fine
        if step < STEPS - 1:
            inner_power = inner_power + power
    found = [total, power, inner_power / (STEPS - 1), inner_sum / (STEPS - 1)]
    current = coarse
    for _ in range(7):
        found.append(current)
        current = current * current
    return found


def mode_table():
    d = np.arange(DEVICES)[:, None]
    lane = np.arange(COLS)[None, :]
    column = lane % LANES
    row = np.where(lane < LANES, d, d + HALF)
    row = np.where(lane == LANES, d, row)
    theta = 2 * np.pi * row / ROWS
    phi = np.where(lane == LANES, np.pi, 2 * np.pi * column / COLS)
    table = np.zeros((DEVICES, TAB_ROWS, COLS))
    for n, value in enumerate(operators(theta, phi)):
        table[:, 3 * n] = value.real
        table[:, 3 * n + 1] = value.real
        table[:, 3 * n + 2] = value.imag
    for at in (0, LANES):
        angle = np.array([0.0 if at == 0 else np.pi])
        first = operators(np.array([0.0]), angle)
        second = operators(np.array([np.pi]), angle)
        for n in range(N_OPS):
            table[0, 3 * n, at] = first[n].real[0]
            table[0, 3 * n + 1, at] = second[n].real[0]
            table[0, 3 * n + 2, at] = 0.0
    return table.astype(np.float32)


def row_table():
    angle = 2 * np.pi * (np.outer(np.arange(HALF), np.arange(HALF)) % ROWS) / ROWS
    return np.concatenate([np.cos(angle), np.sin(angle)], 0).astype(np.float32)


def column_tables():
    c = np.arange(COLS)[:, None]
    n = np.arange(LANES)[None, :]
    angle = 2 * np.pi * ((c * n) % COLS) / COLS
    forward = np.concatenate([np.cos(angle), -np.sin(angle)], 1)
    forward[:, LANES] = np.where(np.arange(COLS) % 2 == 0, 1.0, -1.0)
    backward = 2.0 * forward.T / (ROWS * COLS)
    return forward.astype(np.float32), backward.astype(np.float32)


def dot(a, b):
    return jnp.dot(a, b, precision=HIGHEST, preferred_element_type=jnp.float32)


def swap(x):
    return pltpu.roll(x, LANES, 1)


def lanes_of(shape):
    return lax.broadcasted_iota(jnp.int32, shape, 1)


def alternating(shape):
    return (1 - 2 * (lax.broadcasted_iota(jnp.int32, shape, 0) % 2)).astype(jnp.float32)


def to_pairs(m1a, m1b, m2a, m2b, first_row):
    lane = lanes_of(m1a.shape)
    low = lane < LANES
    edge = (lane % LANES) == 0
    u = jnp.where(low, m1a + swap(m2a), swap(m1b) + m2b)
    v = jnp.where(low, swap(m1a) - m2a, m1b - swap(m2b))
    u = jnp.where(edge, m1a, u)
    v = jnp.where(edge, jnp.where(first_row, m1b, -m2a), v)
    return u, v


def forward_kernel(x_ref, init_ref, col_ref, row_ref, out_ref, init_out_ref):
    y = dot(x_ref[...], col_ref[...])
    sign = alternating(y.shape)
    both = jnp.concatenate([y, y * sign], axis=1)
    m1 = dot(row_ref[:HALF], both)
    m2 = dot(row_ref[HALF:], both)
    first = lax.broadcasted_iota(jnp.int32, y.shape, 0) == 0
    u, v = to_pairs(m1[:, :COLS], m1[:, COLS:], m2[:, :COLS], m2[:, COLS:], first)
    out_ref[pl.ds(0, HALF, stride=2), :] = u
    out_ref[pl.ds(1, HALF, stride=2), :] = v
    group = device_index() // 8 * 8
    yi = dot(init_ref[...], col_ref[...])
    both = jnp.concatenate([yi, yi * sign], axis=1)
    m1 = dot(row_ref[pl.ds(pl.multiple_of(group, 8), 8), :], both)
    m2 = dot(row_ref[pl.ds(pl.multiple_of(HALF + group, 8), 8), :], both)
    first = lax.broadcasted_iota(jnp.int32, (8, COLS), 0) + group == 0
    u, v = to_pairs(m1[:, :COLS], m1[:, COLS:], m2[:, :COLS], m2[:, COLS:], first)
    init_out_ref[:8] = u
    init_out_ref[8:] = v


def device_index():
    return (lax.axis_index("tg") * 32 + lax.axis_index("tc")) * 2 + lax.axis_index("sp")


def shifted(x, distance, fill):
    if distance % 8 == 0:
        return jnp.concatenate([jnp.broadcast_to(fill, (distance, COLS)), x[:-distance]], 0)
    row = lax.broadcasted_iota(jnp.int32, x.shape, 0)
    return jnp.where(row < distance, fill, pltpu.roll(x, distance, 0))


def middle_kernel(got_ref, own_init_ref, other_init_ref, table_ref, out_ref, tab, sem):
    me = device_index()
    copy = pltpu.make_async_copy(table_ref.at[me], tab, sem)
    copy.start()
    sign = (1 - 2 * (me % 2)).astype(jnp.float32)
    part = [got_ref[pl.ds(n, BLOCKS, stride=4), :] for n in range(4)]
    f = (part[0] + sign * part[2], part[1] + sign * part[3])
    place = lax.broadcasted_iota(jnp.int32, (8, COLS), 0) == me % 8
    mine = lambda ref, at: jnp.sum(jnp.where(place, ref[at : at + 8], 0.0), 0, keepdims=True)
    own_scale = jnp.where(me % 2 == 0, 1.0, sign)
    other_scale = jnp.where(me % 2 == 0, sign, 1.0)
    init = tuple(
        own_scale * mine(own_init_ref, at) + other_scale * mine(other_init_ref, at)
        for at in (0, 8)
    )
    copy.wait()

    def apply(n, x):
        on_u, on_v, across = (tab[3 * n + j : 3 * n + j + 1] for j in range(3))
        return on_u * x[0] - across * x[1], across * x[0] + on_v * x[1]

    def add(x, y):
        return x[0] + y[0], x[1] + y[1]

    def moved(x, distance, fill):
        return tuple(shifted(a, distance, b) for a, b in zip(x, fill))

    zero = (jnp.zeros((1, COLS), jnp.float32),) * 2
    w = apply(0, f)
    row = lax.broadcasted_iota(jnp.int32, (BLOCKS, COLS), 0)
    head = apply(4, init)
    t = tuple(a + jnp.where(row == 0, b, 0.0) for a, b in zip(w, head))
    for level in range(7):
        t = add(t, apply(4 + level, moved(t, 1 << level, zero)))
    c = add(w, apply(1, moved(t, 1, init)))
    mean = add(apply(2, moved(c, 1, init)), apply(3, f))
    for n, value in enumerate((*c, *mean)):
        out_ref[pl.ds(n, BLOCKS, stride=8), :] = value
        out_ref[pl.ds(4 + n, BLOCKS, stride=8), :] = value * sign


def backward_kernel(got_ref, col_ref, row_ref, c_ref, mean_ref):
    sign = alternating((HALF, COLS))
    lane = lanes_of((HALF, COLS))
    for n, out in ((0, c_ref), (2, mean_ref)):
        u = got_ref[pl.ds(n, HALF, stride=4), :]
        v = got_ref[pl.ds(n + 1, HALF, stride=4), :]
        both = jnp.concatenate([u, v], axis=1)
        cos = dot(row_ref[:HALF], both)
        sin = dot(row_ref[HALF:], both)
        e = cos[:, :COLS] - sin[:, COLS:]
        f = cos[:, COLS:] + sin[:, :COLS]
        y = jnp.where(lane < LANES, e + sign * swap(e), swap(f) + sign * f)
        y = jnp.where(lane % LANES == 0, e + 0.5 * (sign * v[:1] - u[:1]), y)
        out[...] = dot(y, col_ref[...])


def vmem(n):
    return [pl.BlockSpec(memory_space=pltpu.VMEM)] * n


PARAMS = pltpu.CompilerParams(vmem_limit_bytes=32 * 1024 * 1024)


def shards(initial, source):
    rows = jnp.asarray(row_table())
    forward, backward = (jnp.asarray(a) for a in column_tables())
    table = jnp.asarray(mode_table())
    sds = lambda *shape: jax.ShapeDtypeStruct(shape, jnp.float32)
    sent, own_init = pl.pallas_call(
        forward_kernel,
        out_shape=(sds(2 * DEVICES, COLS), sds(16, COLS)),
        in_specs=vmem(4),
        out_specs=tuple(vmem(2)),
        compiler_params=PARAMS,
    )(source[0], initial, forward, rows)
    other_init = lax.ppermute(own_init, "sp", [(0, 1), (1, 0)])
    got = lax.all_to_all(sent.reshape(DEVICES, 2, COLS), AXES, 0, 0, tiled=True)
    back = pl.pallas_call(
        middle_kernel,
        out_shape=sds(4 * DEVICES, COLS),
        in_specs=vmem(3) + [pl.BlockSpec(memory_space=pl.ANY)],
        out_specs=vmem(1)[0],
        scratch_shapes=[pltpu.VMEM((TAB_ROWS, COLS), jnp.float32), pltpu.SemaphoreType.DMA],
        compiler_params=PARAMS,
    )(got.reshape(2 * DEVICES, COLS), own_init, other_init, table)
    modes = lax.all_to_all(back.reshape(DEVICES, 4, COLS), AXES, 0, 0, tiled=True)
    c_values, block_mean = pl.pallas_call(
        backward_kernel,
        out_shape=(sds(HALF, COLS), sds(HALF, COLS)),
        in_specs=vmem(3),
        out_specs=tuple(vmem(2)),
        compiler_params=PARAMS,
    )(modes.reshape(4 * DEVICES, COLS), backward, rows)
    return c_values[None], block_mean[None]


def solution(mesh):
    in_specs = (P("sp", None), P(("tg", "tc"), "sp", None))
    out_specs = (P(("tg", "tc"), "sp", None), P(("tg", "tc"), "sp", None))
    return jax.shard_map(shards, mesh=mesh, in_specs=in_specs, out_specs=out_specs, check_vma=False)
```

```python
import jax
import jax.numpy as jnp
import numpy as np
from jax import lax
from jax.experimental import pallas as pl
from jax.experimental.pallas import tpu as pltpu
from jax.sharding import PartitionSpec as P

ROWS = 512
HALF = ROWS // 2
COLS = 128
LANES = COLS // 2
STEPS = 16
GROUP = 32
QUAD = 4

fine_center = 0.2
fine_behind = 0.25
fine_ahead = 0.15
coarse_center = 0.04
coarse_behind = 0.31
coarse_ahead = 0.17

HIGHEST = lax.Precision.HIGHEST

GUESS, DEFECT, MEAN_STATE, MEAN_SOURCE, COARSE = 0, 1, 2, 3, 4
LAST = 10
INIT_T, INIT_C = 11, 12
N_OPS = 13


def symbol(theta, phi, center, behind, ahead):
    return (
        center
        + behind * np.exp(-1j * theta)
        + ahead * np.exp(1j * theta)
        + behind * np.exp(-1j * phi)
        + ahead * np.exp(1j * phi)
    )


def operators(theta, phi):
    fine = symbol(theta, phi, fine_center, fine_behind, fine_ahead)
    coarse = symbol(theta, phi, coarse_center, coarse_behind, coarse_ahead)
    power, total = np.ones_like(fine), np.zeros_like(fine)
    inner_sum = np.zeros_like(fine)
    inner_power = np.zeros_like(fine)
    for step in range(STEPS):
        total = total + power
        if step < STEPS - 1:
            inner_sum = inner_sum + total
        power = power * fine
        if step < STEPS - 1:
            inner_power = inner_power + power
    found = [total, power, inner_power / (STEPS - 1), inner_sum / (STEPS - 1)]
    found += [coarse ** (1 << n) for n in range(6)]
    found.append(power * coarse ** (GROUP - 1))
    by_group = []
    for x in range(4):
        from_start = power * coarse ** (GROUP * x - 1) if x else np.ones_like(fine)
        by_group.append(np.stack(found + [coarse ** (GROUP * x), from_start]))
    return np.stack(by_group)


def slice_rows():
    core = np.arange(2)[:, None, None]
    q = np.arange(GROUP)[None, :, None]
    return 2 * (QUAD * q + np.arange(QUAD)[None, None, :]) + core


def mode_table():
    d = slice_rows()[..., None]
    lane = np.arange(COLS)
    row = np.where(lane > LANES, d + HALF, d)
    theta = 2 * np.pi * row / ROWS
    phi = np.where(lane == LANES, np.pi, 2 * np.pi * (lane % LANES) / COLS)
    value = operators(theta, phi + 0 * theta)
    on_u, on_v, across = value.real.copy(), value.real.copy(), value.imag.copy()
    for at, angle in ((0, 0.0), (LANES, np.pi)):
        on_u[:, :, 0, 0, 0, at] = operators(np.array(0.0), np.array(angle)).real
        on_v[:, :, 0, 0, 0, at] = operators(np.array(np.pi), np.array(angle)).real
        across[:, :, 0, 0, 0, at] = 0.0
    table = np.concatenate([on_u, on_v, -across, across], axis=4)
    table = np.moveaxis(table, 1, 3)
    return table.reshape(4, 2, GROUP, 16 * N_OPS, COLS).astype(np.float32)


def row_table():
    turns = slice_rows()[..., None] * np.arange(HALF) % ROWS
    angle = 2 * np.pi * turns / ROWS
    table = np.concatenate([np.cos(angle), np.sin(angle)], axis=2)
    return table.reshape(2, HALF, HALF).astype(np.float32)


def column_tables():
    c = np.arange(COLS)[:, None]
    n = np.arange(LANES)[None, :]
    angle = 2 * np.pi * ((c * n) % COLS) / COLS
    forward = np.concatenate([np.cos(angle), -np.sin(angle)], 1)
    forward[:, LANES] = np.where(np.arange(COLS) % 2 == 0, 1.0, -1.0)
    backward = 2.0 * forward.T / (ROWS * COLS)
    return forward.astype(np.float32), backward.astype(np.float32)


def dot(a, b):
    return jnp.dot(a, b, precision=HIGHEST, preferred_element_type=jnp.float32)


def swap(x):
    return pltpu.roll(x, LANES, x.ndim - 1)


def flip(x):
    return pltpu.roll(x, QUAD, x.ndim - 2)


def tiles(x):
    return x.reshape(x.shape[0] // 8, 8, x.shape[1])


def iota(shape, dim):
    return lax.broadcasted_iota(jnp.int32, shape, dim)


def alternating(shape):
    return (1 - 2 * (iota(shape, 0) % 2)).astype(jnp.float32)


def prepare_kernel(src, init, rows, rows_t, table, src_o, init_o, rows_o, rows_t_o, table_o, sems):
    core = lax.axis_index("sp")
    pairs = (
        (src, src_o),
        (rows.at[core], rows_o),
        (init, init_o),
        (table.at[lax.axis_index("tg"), core, lax.axis_index("tc")], table_o),
        (rows_t.at[core], rows_t_o),
    )
    copies = [pltpu.make_async_copy(a, b, sems.at[n]) for n, (a, b) in enumerate(pairs)]
    for copy in copies:
        copy.start()
    for copy in copies:
        copy.wait()


def to_modes(product, first):
    a, b = tiles(product[:, :COLS]), tiles(product[:, COLS:])
    sub = iota(a.shape, 1)
    lane = iota(a.shape, 2)
    sign = jnp.where(sub < QUAD, 1.0, -1.0)
    own = sign * a
    b_flip = flip(b)
    result = jnp.where(lane < LANES, own + swap(flip(a)), swap(sign * b) + b_flip)
    edge = lane % LANES == 0
    zero_mode = jnp.logical_and(first, jnp.logical_and(iota(a.shape, 0) == 0, sub == QUAD))
    result = jnp.where(edge, jnp.where(zero_mode, b_flip, own), result)
    return result.reshape(product.shape[0], COLS)


def forward_kernel(src, src_other, init, init_other, col, rows, out, init_out):
    core = lax.axis_index("sp")
    own_sign = (1 - 2 * core).astype(jnp.float32)
    sign = alternating((HALF, COLS))

    def columns(own, other):
        y = dot(own_sign * own[...] + other[...], col[...])
        return jnp.concatenate([y, y * sign], axis=1)

    out[...] = to_modes(dot(rows[...], columns(src, src_other)), core == 0)
    at = lax.axis_index("tc")
    own_rows = rows[pl.ds(pl.multiple_of(8 * at, 8), 8), :]
    product = dot(own_rows, columns(init, init_other))
    init_out[...] = to_modes(product, jnp.logical_and(core == 0, at == 0))


class Operators:
    def __init__(self, table):
        self.table = table

    def __call__(self, n, x):
        itself, partner = (self.table[16 * n + j : 16 * n + j + 8] for j in (0, 8))
        return itself * x + partner * flip(x)


def scan_kernel(got, table, c_out, mean_out, message):
    op = Operators(table)
    f = tiles(got[...])
    w = op(GUESS, f)
    t = w
    for level in range(5):
        d = 1 << level
        t = jnp.concatenate([t[:d], t[d:] + op(COARSE + level, t[:-d])], 0)
    c = jnp.concatenate([w[:1], w[1:] + op(DEFECT, t[:-1])], 0)
    source_part = op(MEAN_SOURCE, f)
    mean = jnp.concatenate([source_part[:1], source_part[1:] + op(MEAN_STATE, c[:-1])], 0)
    c_out[...] = c.reshape(HALF, COLS)
    mean_out[...] = mean.reshape(HALF, COLS)
    message[:8] = t[GROUP - 1]
    message[8:] = c[GROUP - 1]


def join_kernel(own, other, table, message, kept):
    op = Operators(table)
    later = lax.axis_index("tg") % 2 == 1
    mine, mine_c, theirs, theirs_c = own[:8], own[8:], other[:8], other[8:]
    prefix = jnp.where(later, theirs, 0.0)
    low = jnp.where(later, theirs, mine)
    high = jnp.where(later, mine, theirs)
    message[:8] = op(COARSE + 5, low) + high
    message[8:] = mine_c + op(LAST, prefix)
    kept[:8] = prefix
    kept[8:] = jnp.where(later, theirs_c, 0.0)


def finish_kernel(c_in, mean_in, kept, other, init, table, out):
    op = Operators(table)
    x = lax.axis_index("tg")
    second = x >= 2
    at_start = x % 2 == 0
    low = jnp.where(second, other[:8], 0.0)
    low_c = jnp.where(second, other[8:], 0.0)
    init_v = init[...]
    carry = kept[:8] + jnp.where(at_start, low, op(COARSE + 5, low)) + op(INIT_T, init_v)
    before = kept[8:] + jnp.where(at_start, low_c, op(LAST, low)) + op(INIT_C, init_v)
    spread = carry[None]
    for level in range(5):
        spread = jnp.concatenate([spread, op(COARSE + level, spread)], 0)
    added = op(DEFECT, spread)
    c = tiles(c_in[...]) + added
    shift = jnp.concatenate([before[None], added[:-1]], 0)
    mean = tiles(mean_in[...]) + op(MEAN_STATE, shift)
    out[:, :8] = c
    out[:, 8:] = mean


def backward_kernel(got, rows_t, col, out, own_out):
    core = lax.axis_index("sp")
    got_v = got[...]
    parts = [got_v[:, :8], got_v[:, 8:]]
    sub = iota(parts[0].shape, 1)
    flat = lambda v: v.reshape(HALF, COLS)
    left = [flat(jnp.where(sub < QUAD, v, -v)) for v in parts]
    right = [flat(flip(v)) for v in parts]
    product = dot(rows_t[...], jnp.concatenate(left + right, axis=1))
    sign = alternating((HALF, COLS))
    lane = iota((HALF, COLS), 1)
    own_sign = (1 - 2 * core).astype(jnp.float32)
    zero_mode = jnp.where(core == 0, 0.5, 0.0)
    for n, v in enumerate(parts):
        e = product[:, COLS * n : COLS * (n + 1)]
        f = product[:, COLS * (n + 2) : COLS * (n + 3)]
        y = jnp.where(lane < LANES, e + sign * swap(e), swap(f) + sign * f)
        first_u, first_v = v[0, :1], v[0, QUAD : QUAD + 1]
        edge = e + zero_mode * (sign * first_v - first_u)
        part = dot(jnp.where(lane % LANES == 0, edge, y), col[...])
        out[n] = part
        own_out[n] = own_sign * part


PARAMS = pltpu.CompilerParams(vmem_limit_bytes=32 * 1024 * 1024)


def call(kernel, shapes, args, hbm=False, scratch=()):
    space = pltpu.HBM if hbm else pltpu.VMEM
    return pl.pallas_call(
        kernel,
        out_shape=[jax.ShapeDtypeStruct(s, jnp.float32) for s in shapes],
        in_specs=[pl.BlockSpec(memory_space=space)] * len(args),
        out_specs=[pl.BlockSpec(memory_space=pltpu.VMEM)] * len(shapes),
        scratch_shapes=scratch,
        compiler_params=PARAMS,
    )(*args)


def shards(initial, source):
    rows = row_table()
    forward, backward = column_tables()
    own = source[0]
    swap_cores = [(0, 1), (1, 0)]
    src_other = lax.ppermute(own, "sp", swap_cores)
    init_other = lax.ppermute(initial, "sp", swap_cores)
    block = (HALF, COLS)
    square = (HALF, HALF)
    src, init, rows_v, rows_t_v, table = call(
        prepare_kernel,
        [block, block, square, square, (16 * N_OPS, COLS)],
        [own, initial, rows, rows.transpose(0, 2, 1).copy(), mode_table()],
        hbm=True,
        scratch=[pltpu.SemaphoreType.DMA((5,))],
    )
    tile, two = (8, COLS), (16, COLS)
    sent, init_modes = call(
        forward_kernel, [block, tile], [src, src_other, init, init_other, forward, rows_v]
    )
    got = lax.all_to_all(sent.reshape(GROUP, 8, COLS), "tc", 0, 0, tiled=True)
    c, mean, message = call(scan_kernel, [block, block, two], [got.reshape(block), table])
    other = lax.ppermute(message, "tg", [(i, i ^ 1) for i in range(4)])
    message, kept = call(join_kernel, [two, two], [message, other, table])
    other = lax.ppermute(message, "tg", [(i, 3 - i) for i in range(4)])
    (back,) = call(
        finish_kernel, [(GROUP, 16, COLS)], [c, mean, kept, other, init_modes, table]
    )
    modes = lax.all_to_all(back, "tc", 0, 0, tiled=True)
    part, own_part = call(
        backward_kernel, [(2, HALF, COLS), (2, HALF, COLS)], [modes, rows_t_v, backward]
    )
    other_part = lax.ppermute(part, "sp", swap_cores)
    return own_part[:1] + other_part[:1], own_part[1:] + other_part[1:]


def solution(mesh):
    in_specs = (P("sp", None), P(("tg", "tc"), "sp", None))
    out_specs = (P(("tg", "tc"), "sp", None), P(("tg", "tc"), "sp", None))
    return jax.shard_map(shards, mesh=mesh, in_specs=in_specs, out_specs=out_specs, check_vma=False)
```

```python
import jax
import jax.numpy as jnp
import numpy as np
from jax import lax
from jax.experimental import pallas as pl
from jax.experimental.pallas import tpu as pltpu
from jax.sharding import PartitionSpec as P

ROWS = 512
HALF = ROWS // 2
COLS = 128
LANES = COLS // 2
STEPS = 16
GROUP = 32
QUAD = 4

fine_center = 0.2
fine_behind = 0.25
fine_ahead = 0.15
coarse_center = 0.04
coarse_behind = 0.31
coarse_ahead = 0.17

HIGHEST = lax.Precision.HIGHEST

MESH_SHAPE = (4, 2, 2, 2, 4, 2)
MESH_AXES = ("x", "zh", "z1", "z0", "y", "sp")
PLANE = ("x", "z0", "y")
RUN = 8

GUESS, DEFECT, MEAN_STATE, MEAN_SOURCE, COARSE = 0, 1, 2, 3, 4
LAST_8, LAST_16, LAST_32 = 10, 11, 12
N_OPS = 13


def symbol(theta, phi, center, behind, ahead):
    return (
        center
        + behind * np.exp(-1j * theta)
        + ahead * np.exp(1j * theta)
        + behind * np.exp(-1j * phi)
        + ahead * np.exp(1j * phi)
    )


def operators(theta, phi):
    fine = symbol(theta, phi, fine_center, fine_behind, fine_ahead)
    coarse = symbol(theta, phi, coarse_center, coarse_behind, coarse_ahead)
    power, total = np.ones_like(fine), np.zeros_like(fine)
    inner_sum = np.zeros_like(fine)
    inner_power = np.zeros_like(fine)
    for step in range(STEPS):
        total = total + power
        if step < STEPS - 1:
            inner_sum = inner_sum + total
        power = power * fine
        if step < STEPS - 1:
            inner_power = inner_power + power
    found = [total, power, inner_power / (STEPS - 1), inner_sum / (STEPS - 1)]
    found += [coarse ** (1 << n) for n in range(6)]
    found += [power * coarse ** (n - 1) for n in (8, 16, 32)]
    return np.stack(found)


def slice_rows():
    core = np.arange(2)[:, None, None]
    q = np.arange(GROUP)[None, :, None]
    return 2 * (QUAD * q + np.arange(QUAD)[None, None, :]) + core


def mode_table():
    d = slice_rows()[..., None]
    lane = np.arange(COLS)
    row = np.where(lane > LANES, d + HALF, d)
    theta = 2 * np.pi * row / ROWS
    phi = np.where(lane == LANES, np.pi, 2 * np.pi * (lane % LANES) / COLS)
    value = operators(theta, phi + 0 * theta)
    on_u, on_v, across = value.real.copy(), value.real.copy(), value.imag.copy()
    for at, angle in ((0, 0.0), (LANES, np.pi)):
        on_u[:, 0, 0, 0, at] = operators(np.array(0.0), np.array(angle)).real
        on_v[:, 0, 0, 0, at] = operators(np.array(np.pi), np.array(angle)).real
        across[:, 0, 0, 0, at] = 0.0
    table = np.concatenate([on_u, on_v, -across, across], axis=3)
    table = np.moveaxis(table, 0, 2)
    return table.reshape(2, GROUP, 16 * N_OPS, COLS).astype(np.float32)


def row_table():
    turns = slice_rows()[..., None] * np.arange(HALF) % ROWS
    angle = 2 * np.pi * turns / ROWS
    table = np.concatenate([np.cos(angle), np.sin(angle)], axis=2)
    return table.reshape(2, HALF, HALF).astype(np.float32)


def column_tables():
    c = np.arange(COLS)[:, None]
    n = np.arange(LANES)[None, :]
    angle = 2 * np.pi * ((c * n) % COLS) / COLS
    forward = np.concatenate([np.cos(angle), -np.sin(angle)], 1)
    forward[:, LANES] = np.where(np.arange(COLS) % 2 == 0, 1.0, -1.0)
    backward = 2.0 * forward.T / (ROWS * COLS)
    return forward.astype(np.float32), backward.astype(np.float32)


def dot(a, b):
    return jnp.dot(a, b, precision=HIGHEST, preferred_element_type=jnp.float32)


def swap(x):
    return pltpu.roll(x, LANES, x.ndim - 1)


def flip(x):
    return pltpu.roll(x, QUAD, x.ndim - 2)


def tiles(x):
    return x.reshape(x.shape[0] // 8, 8, x.shape[1])


def iota(shape, dim):
    return lax.broadcasted_iota(jnp.int32, shape, dim)


def alternating(shape):
    return (1 - 2 * (iota(shape, 0) % 2)).astype(jnp.float32)


def prepare_kernel(src, init, rows, rows_t, table, src_o, init_o, rows_o, rows_t_o, table_o, sems):
    core = lax.axis_index("sp")
    pairs = (
        (src, src_o),
        (rows.at[core], rows_o),
        (init, init_o),
        (table.at[core, own_slice()], table_o),
        (rows_t.at[core], rows_t_o),
    )
    copies = [pltpu.make_async_copy(a, b, sems.at[n]) for n, (a, b) in enumerate(pairs)]
    for copy in copies:
        copy.start()
    for copy in copies:
        copy.wait()


def to_modes(product, first):
    a, b = tiles(product[:, :COLS]), tiles(product[:, COLS:])
    sub = iota(a.shape, 1)
    lane = iota(a.shape, 2)
    sign = jnp.where(sub < QUAD, 1.0, -1.0)
    own = sign * a
    b_flip = flip(b)
    result = jnp.where(lane < LANES, own + swap(flip(a)), swap(sign * b) + b_flip)
    edge = lane % LANES == 0
    zero_mode = jnp.logical_and(first, jnp.logical_and(iota(a.shape, 0) == 0, sub == QUAD))
    result = jnp.where(edge, jnp.where(zero_mode, b_flip, own), result)
    return result.reshape(product.shape[0], COLS)


def own_slice():
    return lax.axis_index("x") * 8 + lax.axis_index("z0") * 4 + lax.axis_index("y")


def columns(own, other, col):
    own_sign = (1 - 2 * lax.axis_index("sp")).astype(jnp.float32)
    y = dot(own_sign * own[...] + other[...], col[...])
    return jnp.concatenate([y, y * alternating(y.shape)], axis=1)


def forward_kernel(src, src_other, col, rows, out):
    first = lax.axis_index("sp") == 0
    out[...] = to_modes(dot(rows[...], columns(src, src_other, col)), first)


def initial_kernel(init, init_other, col, rows, out):
    at = own_slice()
    own_rows = rows[pl.ds(pl.multiple_of(8 * at, 8), 8), :]
    first = jnp.logical_and(lax.axis_index("sp") == 0, at == 0)
    out[...] = to_modes(dot(own_rows, columns(init, init_other, col)), first)


class Operators:
    def __init__(self, table):
        self.table = table

    def __call__(self, n, x):
        itself, partner = (self.table[16 * n + j : 16 * n + j + 8] for j in (0, 8))
        return itself * x + partner * flip(x)


def after(first, rest):
    return jnp.concatenate([first, rest], axis=1)


def place():
    return 2 * lax.axis_index("zh") + lax.axis_index("z1")


def scan_kernel(got, table, c_out, mean_out, message):
    op = Operators(table)
    f = got[...].reshape(4, RUN, 8, COLS)
    w = op(GUESS, f)
    t = w
    for level in range(3):
        d = 1 << level
        t = after(t[:, :d], t[:, d:] + op(COARSE + level, t[:, :-d]))
    c = after(w[:, :1], w[:, 1:] + op(DEFECT, t[:, :-1]))
    source_part = op(MEAN_SOURCE, f)
    c_out[...] = c
    mean_out[...] = after(source_part[:, :1], source_part[:, 1:] + op(MEAN_STATE, c[:, :-1]))
    message[0] = t[:, RUN - 1]
    message[1] = c[:, RUN - 1]


def join_kernel(own, other, table, message, kept):
    op = Operators(table)
    later = lax.axis_index("z1") == 1
    mine, theirs = own[0], other[0]
    prefix = jnp.where(later, theirs, 0.0)
    low = jnp.where(later, theirs, mine)
    high = jnp.where(later, mine, theirs)
    message[0] = op(COARSE + 3, low) + high
    message[1] = own[1] + op(LAST_8, prefix)
    kept[0] = prefix
    kept[1] = jnp.where(later, other[1], 0.0)


def finish_kernel(c_in, mean_in, kept, own, other, init, table, out):
    op = Operators(table)
    at = place()
    second = at >= 2
    at_start = at % 2 == 0
    mine, theirs, theirs_c = own[0], other[0], other[1]
    low = jnp.where(second, theirs, mine)
    high = jnp.where(second, mine, theirs)
    total = op(COARSE + 4, low) + high
    state = [init[...]]
    for x in range(3):
        state.append(op(COARSE + 5, state[x]) + total[x])
    state = jnp.stack(state)
    part = jnp.where(second, low, 0.0)
    part_c = jnp.where(second, theirs_c, 0.0)
    carry = kept[0] + jnp.where(at_start, part, op(COARSE + 3, part))
    before = kept[1] + jnp.where(at_start, part_c, op(LAST_8, part))
    by_8, by_16 = op(COARSE + 3, state), op(COARSE + 4, state)
    by_24 = op(COARSE + 3, by_16)
    carry = carry + jnp.where(
        at == 0, state, jnp.where(at == 1, by_8, jnp.where(at == 2, by_16, by_24))
    )
    to_last = jnp.where(at == 1, state, jnp.where(at == 2, by_8, by_16))
    before = before + op(LAST_8, to_last)
    ends = theirs_c[:3] + op(LAST_16, low[:3]) + op(LAST_32, state[:3])
    before = jnp.where(at == 0, jnp.concatenate([init[...][None], ends], axis=0), before)
    spread = carry[:, None]
    for level in range(3):
        spread = after(spread, op(COARSE + level, spread))
    added = op(DEFECT, spread)
    shift = after(before[:, None], added[:, :-1])
    c = c_in[...] + added
    mean = mean_in[...] + op(MEAN_STATE, shift)
    out[:, :8] = c.reshape(GROUP, 8, COLS)
    out[:, 8:] = mean.reshape(GROUP, 8, COLS)


def backward_kernel(got, rows_t, col, out, own_out):
    core = lax.axis_index("sp")
    got_v = got[...]
    parts = [got_v[:, :8], got_v[:, 8:]]
    sub = iota(parts[0].shape, 1)
    flat = lambda v: v.reshape(HALF, COLS)
    left = [flat(jnp.where(sub < QUAD, v, -v)) for v in parts]
    right = [flat(flip(v)) for v in parts]
    product = dot(rows_t[...], jnp.concatenate(left + right, axis=1))
    sign = alternating((HALF, COLS))
    lane = iota((HALF, COLS), 1)
    own_sign = (1 - 2 * core).astype(jnp.float32)
    zero_mode = jnp.where(core == 0, 0.5, 0.0)
    for n, v in enumerate(parts):
        e = product[:, COLS * n : COLS * (n + 1)]
        f = product[:, COLS * (n + 2) : COLS * (n + 3)]
        y = jnp.where(lane < LANES, e + sign * swap(e), swap(f) + sign * f)
        first_u, first_v = v[0, :1], v[0, QUAD : QUAD + 1]
        edge = e + zero_mode * (sign * first_v - first_u)
        part = dot(jnp.where(lane % LANES == 0, edge, y), col[...])
        out[n] = part
        own_out[n] = own_sign * part


PARAMS = pltpu.CompilerParams(vmem_limit_bytes=32 * 1024 * 1024)


def call(kernel, shapes, args, hbm=False, scratch=()):
    space = pltpu.HBM if hbm else pltpu.VMEM
    return pl.pallas_call(
        kernel,
        out_shape=[jax.ShapeDtypeStruct(s, jnp.float32) for s in shapes],
        in_specs=[pl.BlockSpec(memory_space=space)] * len(args),
        out_specs=[pl.BlockSpec(memory_space=pltpu.VMEM)] * len(shapes),
        scratch_shapes=scratch,
        compiler_params=PARAMS,
    )(*args)


def shards(initial, source):
    rows = row_table()
    forward, backward = column_tables()
    own = source[0]
    swap_two = [(0, 1), (1, 0)]
    src_other = lax.ppermute(own, "sp", swap_two)
    block = (HALF, COLS)
    square = (HALF, HALF)
    constants = [rows, rows.transpose(0, 2, 1).copy(), mode_table()]
    args = [own, initial, *(jnp.asarray(a) for a in constants)]
    src, init, rows_v, rows_t_v, table = call(
        prepare_kernel,
        [block, block, square, square, (16 * N_OPS, COLS)],
        [pltpu.with_memory_space_constraint(a, pltpu.HBM) for a in args],
        hbm=True,
        scratch=[pltpu.SemaphoreType.DMA((5,))],
    )
    (sent,) = call(forward_kernel, [block], [src, src_other, forward, rows_v])
    got = lax.all_to_all(sent.reshape(GROUP, 8, COLS), PLANE, 0, 0, tiled=True)
    runs, ends = (4, RUN, 8, COLS), (2, 4, 8, COLS)
    c, mean, message = call(scan_kernel, [runs, runs, ends], [got, table])
    initial, message = lax.optimization_barrier((initial, message))
    other = lax.ppermute(message, "z1", swap_two)
    init_other = lax.ppermute(initial, "sp", swap_two)
    (init_modes,) = call(initial_kernel, [(8, COLS)], [init, init_other, forward, rows_v])
    message, kept = call(join_kernel, [ends, ends], [message, other, table])
    other = lax.ppermute(message, ("zh", "z1"), [(i, 3 - i) for i in range(4)])
    (back,) = call(
        finish_kernel,
        [(GROUP, 16, COLS)],
        [c, mean, kept, message, other, init_modes, table],
    )
    modes = lax.all_to_all(back, PLANE, 0, 0, tiled=True)
    part, own_part = call(
        backward_kernel, [(2, HALF, COLS), (2, HALF, COLS)], [modes, rows_t_v, backward]
    )
    other_part = lax.ppermute(part, "sp", swap_two)
    return own_part[:1] + other_part[:1], own_part[1:] + other_part[1:]


def solution(mesh):
    mesh = jax.sharding.Mesh(mesh.devices.reshape(MESH_SHAPE), MESH_AXES)
    by_block = P(MESH_AXES[:-1], "sp", None)
    return jax.shard_map(
        shards,
        mesh=mesh,
        in_specs=(P("sp", None), by_block),
        out_specs=(by_block, by_block),
        check_vma=False,
    )
```

```python
import jax
import jax.numpy as jnp
import numpy as np
from jax import lax
from jax.experimental import pallas as pl
from jax.experimental.pallas import tpu as pltpu
from jax.sharding import PartitionSpec as P

ROWS = 512
HALF = ROWS // 2
COLS = 128
LANES = COLS // 2
STEPS = 16
GROUP = 32
QUAD = 4

fine_center = 0.2
fine_behind = 0.25
fine_ahead = 0.15
coarse_center = 0.04
coarse_behind = 0.31
coarse_ahead = 0.17

HIGHEST = lax.Precision.HIGHEST

MESH_SHAPE = (4, 2, 2, 2, 4, 2)
MESH_AXES = ("x", "zh", "z1", "z0", "y", "sp")
PLANE = ("x", "z0", "y")
RUN = 8

GUESS, DEFECT, MEAN_STATE, MEAN_SOURCE, COARSE = 0, 1, 2, 3, 4
LAST_8, LAST_16, LAST_32 = 10, 11, 12
N_OPS = 13


def symbol(theta, phi, center, behind, ahead):
    return (
        center
        + behind * np.exp(-1j * theta)
        + ahead * np.exp(1j * theta)
        + behind * np.exp(-1j * phi)
        + ahead * np.exp(1j * phi)
    )


def operators(theta, phi):
    fine = symbol(theta, phi, fine_center, fine_behind, fine_ahead)
    coarse = symbol(theta, phi, coarse_center, coarse_behind, coarse_ahead)
    power, total = np.ones_like(fine), np.zeros_like(fine)
    inner_sum = np.zeros_like(fine)
    inner_power = np.zeros_like(fine)
    for step in range(STEPS):
        total = total + power
        if step < STEPS - 1:
            inner_sum = inner_sum + total
        power = power * fine
        if step < STEPS - 1:
            inner_power = inner_power + power
    found = [total, power, inner_power / (STEPS - 1), inner_sum / (STEPS - 1)]
    found += [coarse ** (1 << n) for n in range(6)]
    found += [power * coarse ** (n - 1) for n in (8, 16, 32)]
    return np.stack(found)


def slice_rows():
    core = np.arange(2)[:, None, None]
    q = np.arange(GROUP)[None, :, None]
    return 2 * (QUAD * q + np.arange(QUAD)[None, None, :]) + core


def mode_table():
    d = slice_rows()[..., None]
    lane = np.arange(COLS)
    row = np.where(lane > LANES, d + HALF, d)
    theta = 2 * np.pi * row / ROWS
    phi = np.where(lane == LANES, np.pi, 2 * np.pi * (lane % LANES) / COLS)
    value = operators(theta, phi + 0 * theta)
    on_u, on_v, across = value.real.copy(), value.real.copy(), value.imag.copy()
    for at, angle in ((0, 0.0), (LANES, np.pi)):
        on_u[:, 0, 0, 0, at] = operators(np.array(0.0), np.array(angle)).real
        on_v[:, 0, 0, 0, at] = operators(np.array(np.pi), np.array(angle)).real
        across[:, 0, 0, 0, at] = 0.0
    table = np.concatenate([on_u, on_v, -across, across], axis=3)
    table = np.moveaxis(table, 0, 2)
    return table.reshape(2, GROUP, 16 * N_OPS, COLS).astype(np.float32)


def row_table():
    turns = slice_rows()[..., None] * np.arange(HALF) % ROWS
    angle = 2 * np.pi * turns / ROWS
    table = np.concatenate([np.cos(angle), np.sin(angle)], axis=2)
    return table.reshape(2, HALF, HALF).astype(np.float32)


def column_tables():
    c = np.arange(COLS)[:, None]
    n = np.arange(LANES)[None, :]
    angle = 2 * np.pi * ((c * n) % COLS) / COLS
    forward = np.concatenate([np.cos(angle), -np.sin(angle)], 1)
    forward[:, LANES] = np.where(np.arange(COLS) % 2 == 0, 1.0, -1.0)
    backward = 2.0 * forward.T / (ROWS * COLS)
    return forward.astype(np.float32), backward.astype(np.float32)


def dot(a, b):
    return jnp.dot(a, b, precision=HIGHEST, preferred_element_type=jnp.float32)


def swap(x):
    return pltpu.roll(x, LANES, x.ndim - 1)


def flip(x):
    return pltpu.roll(x, QUAD, x.ndim - 2)


def tiles(x):
    return x.reshape(x.shape[0] // 8, 8, x.shape[1])


def iota(shape, dim):
    return lax.broadcasted_iota(jnp.int32, shape, dim)


def alternating(shape):
    return (1 - 2 * (iota(shape, 0) % 2)).astype(jnp.float32)


def parity():
    return (lax.axis_index("sp") + lax.axis_index("z1")) % 2


def prepare_kernel(src, init, rows, rows_t, table, src_o, init_o, rows_o, rows_t_o, table_o, sems):
    kind = parity()
    pairs = (
        (src, src_o),
        (rows.at[kind], rows_o),
        (init, init_o),
        (table.at[kind, own_slice()], table_o),
        (rows_t.at[kind], rows_t_o),
    )
    copies = [pltpu.make_async_copy(a, b, sems.at[n]) for n, (a, b) in enumerate(pairs)]
    for copy in copies:
        copy.start()
    for copy in copies:
        copy.wait()


def to_modes(product, first):
    a, b = tiles(product[:, :COLS]), tiles(product[:, COLS:])
    sub = iota(a.shape, 1)
    lane = iota(a.shape, 2)
    sign = jnp.where(sub < QUAD, 1.0, -1.0)
    own = sign * a
    b_flip = flip(b)
    result = jnp.where(lane < LANES, own + swap(flip(a)), swap(sign * b) + b_flip)
    edge = lane % LANES == 0
    zero_mode = jnp.logical_and(first, jnp.logical_and(iota(a.shape, 0) == 0, sub == QUAD))
    result = jnp.where(edge, jnp.where(zero_mode, b_flip, own), result)
    return result.reshape(product.shape[0], COLS)


def own_slice():
    return lax.axis_index("x") * 8 + lax.axis_index("z0") * 4 + lax.axis_index("y")


def fold(own, other):
    odd, lower = parity() == 1, lax.axis_index("sp") == 1
    own_sign = jnp.where(jnp.logical_and(odd, lower), -1.0, 1.0)
    other_sign = jnp.where(jnp.logical_and(odd, jnp.logical_not(lower)), -1.0, 1.0)
    return own_sign * own[...] + other_sign * other[...]


def columns(folded, col):
    y = dot(folded, col[...])
    return jnp.concatenate([y, y * alternating(y.shape)], axis=1)


def forward_kernel(src, src_other, init, init_other, col, rows, out, init_out):
    first = parity() == 0
    out[...] = to_modes(dot(rows[...], columns(fold(src, src_other), col)), first)
    init_out[...] = fold(init, init_other)


def initial_kernel(folded, col, rows, out):
    at = own_slice()
    own_rows = rows[pl.ds(pl.multiple_of(8 * at, 8), 8), :]
    first = jnp.logical_and(parity() == 0, at == 0)
    out[...] = to_modes(dot(own_rows, columns(folded[...], col)), first)


class Operators:
    def __init__(self, table):
        self.table = table

    def __call__(self, n, x):
        itself, partner = (self.table[16 * n + j : 16 * n + j + 8] for j in (0, 8))
        return itself * x + partner * flip(x)


def after(first, rest):
    return jnp.concatenate([first, rest], axis=1)


def place():
    return 2 * lax.axis_index("zh") + lax.axis_index("z1")


def scan_kernel(got, table, c_out, mean_out, message):
    op = Operators(table)
    f = got[...].reshape(4, RUN, 8, COLS)
    w = op(GUESS, f)
    t = w
    for level in range(3):
        d = 1 << level
        t = after(t[:, :d], t[:, d:] + op(COARSE + level, t[:, :-d]))
    c = after(w[:, :1], w[:, 1:] + op(DEFECT, t[:, :-1]))
    source_part = op(MEAN_SOURCE, f)
    c_out[...] = c
    mean_out[...] = after(source_part[:, :1], source_part[:, 1:] + op(MEAN_STATE, c[:, :-1]))
    message[0] = t[:, RUN - 1]
    message[1] = c[:, RUN - 1]


def join_kernel(own, other, table, message, kept):
    op = Operators(table)
    later = lax.axis_index("z1") == 1
    mine, theirs = own[0], other[0]
    prefix = jnp.where(later, theirs, 0.0)
    low = jnp.where(later, theirs, mine)
    high = jnp.where(later, mine, theirs)
    message[0] = op(COARSE + 3, low) + high
    message[1] = own[1] + op(LAST_8, prefix)
    kept[0] = prefix
    kept[1] = jnp.where(later, other[1], 0.0)


def finish_kernel(c_in, mean_in, kept, own, other, init, table, out):
    op = Operators(table)
    at = place()
    second = at >= 2
    at_start = at % 2 == 0
    mine, theirs, theirs_c = own[0], other[0], other[1]
    low = jnp.where(second, theirs, mine)
    high = jnp.where(second, mine, theirs)
    total = op(COARSE + 4, low) + high
    state = [init[...]]
    for x in range(3):
        state.append(op(COARSE + 5, state[x]) + total[x])
    state = jnp.stack(state)
    part = jnp.where(second, low, 0.0)
    part_c = jnp.where(second, theirs_c, 0.0)
    carry = kept[0] + jnp.where(at_start, part, op(COARSE + 3, part))
    before = kept[1] + jnp.where(at_start, part_c, op(LAST_8, part))
    by_8, by_16 = op(COARSE + 3, state), op(COARSE + 4, state)
    by_24 = op(COARSE + 3, by_16)
    carry = carry + jnp.where(
        at == 0, state, jnp.where(at == 1, by_8, jnp.where(at == 2, by_16, by_24))
    )
    to_last = jnp.where(at == 1, state, jnp.where(at == 2, by_8, by_16))
    before = before + op(LAST_8, to_last)
    ends = theirs_c[:3] + op(LAST_16, low[:3]) + op(LAST_32, state[:3])
    before = jnp.where(at == 0, jnp.concatenate([init[...][None], ends], axis=0), before)
    spread = carry[:, None]
    for level in range(3):
        spread = after(spread, op(COARSE + level, spread))
    added = op(DEFECT, spread)
    shift = after(before[:, None], added[:, :-1])
    c = c_in[...] + added
    mean = mean_in[...] + op(MEAN_STATE, shift)
    out[:, :8] = c.reshape(GROUP, 8, COLS)
    out[:, 8:] = mean.reshape(GROUP, 8, COLS)


def backward_kernel(got, rows_t, col, out, own_out):
    odd, lower = parity() == 1, lax.axis_index("sp") == 1
    got_v = got[...]
    parts = [got_v[:, :8], got_v[:, 8:]]
    sub = iota(parts[0].shape, 1)
    flat = lambda v: v.reshape(HALF, COLS)
    left = [flat(jnp.where(sub < QUAD, v, -v)) for v in parts]
    right = [flat(flip(v)) for v in parts]
    product = dot(rows_t[...], jnp.concatenate(left + right, axis=1))
    sign = alternating((HALF, COLS))
    lane = iota((HALF, COLS), 1)
    own_sign = jnp.where(jnp.logical_and(odd, lower), -1.0, 1.0)
    sent_sign = jnp.where(jnp.logical_and(odd, jnp.logical_not(lower)), -1.0, 1.0)
    zero_mode = jnp.where(odd, 0.0, 0.5)
    for n, v in enumerate(parts):
        e = product[:, COLS * n : COLS * (n + 1)]
        f = product[:, COLS * (n + 2) : COLS * (n + 3)]
        y = jnp.where(lane < LANES, e + sign * swap(e), swap(f) + sign * f)
        first_u, first_v = v[0, :1], v[0, QUAD : QUAD + 1]
        edge = e + zero_mode * (sign * first_v - first_u)
        part = dot(jnp.where(lane % LANES == 0, edge, y), col[...])
        out[n] = sent_sign * part
        own_out[n] = own_sign * part


PARAMS = pltpu.CompilerParams(vmem_limit_bytes=32 * 1024 * 1024)


def call(kernel, shapes, args, hbm=False, scratch=()):
    space = pltpu.HBM if hbm else pltpu.VMEM
    return pl.pallas_call(
        kernel,
        out_shape=[jax.ShapeDtypeStruct(s, jnp.float32) for s in shapes],
        in_specs=[pl.BlockSpec(memory_space=space)] * len(args),
        out_specs=[pl.BlockSpec(memory_space=pltpu.VMEM)] * len(shapes),
        scratch_shapes=scratch,
        compiler_params=PARAMS,
    )(*args)


def shards(initial, source):
    rows = row_table()
    forward, backward = column_tables()
    own = source[0]
    swap_two = [(0, 1), (1, 0)]
    src_other = lax.ppermute(own, "sp", swap_two)
    init_other = lax.ppermute(initial, "sp", swap_two)
    block = (HALF, COLS)
    square = (HALF, HALF)
    constants = [rows, rows.transpose(0, 2, 1).copy(), mode_table()]
    args = [own, initial, *(jnp.asarray(a) for a in constants)]
    src, init, rows_v, rows_t_v, table = call(
        prepare_kernel,
        [block, block, square, square, (16 * N_OPS, COLS)],
        [pltpu.with_memory_space_constraint(a, pltpu.HBM) for a in args],
        hbm=True,
        scratch=[pltpu.SemaphoreType.DMA((5,))],
    )
    sent, folded = call(
        forward_kernel, [block, block], [src, src_other, init, init_other, forward, rows_v]
    )
    got = lax.all_to_all(sent.reshape(GROUP, 8, COLS), PLANE, 0, 0, tiled=True)
    runs, ends = (4, RUN, 8, COLS), (2, 4, 8, COLS)
    c, mean, message = call(scan_kernel, [runs, runs, ends], [got, table])
    folded, message = lax.optimization_barrier((folded, message))
    other = lax.ppermute(message, ("z1", "sp"), [(i, i ^ 3) for i in range(4)])
    (init_modes,) = call(initial_kernel, [(8, COLS)], [folded, forward, rows_v])
    message, kept = call(join_kernel, [ends, ends], [message, other, table])
    other = lax.ppermute(message, ("zh", "z1", "sp"), [(i, i ^ 7) for i in range(8)])
    (back,) = call(
        finish_kernel,
        [(GROUP, 16, COLS)],
        [c, mean, kept, message, other, init_modes, table],
    )
    modes = lax.all_to_all(back, PLANE, 0, 0, tiled=True)
    part, own_part = call(
        backward_kernel, [(2, HALF, COLS), (2, HALF, COLS)], [modes, rows_t_v, backward]
    )
    other_part = lax.ppermute(part, "sp", swap_two)
    return own_part[:1] + other_part[:1], own_part[1:] + other_part[1:]


def solution(mesh):
    mesh = jax.sharding.Mesh(mesh.devices.reshape(MESH_SHAPE), MESH_AXES)
    by_block = P(MESH_AXES[:-1], "sp", None)
    return jax.shard_map(
        shards,
        mesh=mesh,
        in_specs=(P("sp", None), by_block),
        out_specs=(by_block, by_block),
        check_vma=False,
    )
```

```python
import jax
import jax.numpy as jnp
import numpy as np
from jax import lax
from jax.experimental import pallas as pl
from jax.experimental.pallas import tpu as pltpu
from jax.sharding import PartitionSpec as P

ROWS = 512
HALF = ROWS // 2
COLS = 128
LANES = COLS // 2
STEPS = 16
GROUP = 32
QUAD = 4

fine_center = 0.2
fine_behind = 0.25
fine_ahead = 0.15
coarse_center = 0.04
coarse_behind = 0.31
coarse_ahead = 0.17

HIGHEST = lax.Precision.HIGHEST

MESH_SHAPE = (4, 2, 2, 2, 4, 2)
MESH_AXES = ("x", "zh", "z1", "z0", "y", "sp")
PLANE = ("x", "z0", "y")
RUN = 8

GUESS, DEFECT, MEAN_STATE, MEAN_SOURCE, COARSE = 0, 1, 2, 3, 4
LAST_8, LAST_16, LAST_32 = 10, 11, 12
N_OPS = 13


def symbol(theta, phi, center, behind, ahead):
    return (
        center
        + behind * np.exp(-1j * theta)
        + ahead * np.exp(1j * theta)
        + behind * np.exp(-1j * phi)
        + ahead * np.exp(1j * phi)
    )


def operators(theta, phi):
    fine = symbol(theta, phi, fine_center, fine_behind, fine_ahead)
    coarse = symbol(theta, phi, coarse_center, coarse_behind, coarse_ahead)
    power, total = np.ones_like(fine), np.zeros_like(fine)
    inner_sum = np.zeros_like(fine)
    inner_power = np.zeros_like(fine)
    for step in range(STEPS):
        total = total + power
        if step < STEPS - 1:
            inner_sum = inner_sum + total
        power = power * fine
        if step < STEPS - 1:
            inner_power = inner_power + power
    found = [total, power, inner_power / (STEPS - 1), inner_sum / (STEPS - 1)]
    found += [coarse ** (1 << n) for n in range(6)]
    found += [power * coarse ** (n - 1) for n in (8, 16, 32)]
    return np.stack(found)


def slice_rows():
    core = np.arange(2)[:, None, None]
    q = np.arange(GROUP)[None, :, None]
    return 2 * (QUAD * q + np.arange(QUAD)[None, None, :]) + core


def mode_table():
    d = slice_rows()[..., None]
    lane = np.arange(COLS)
    row = np.where(lane > LANES, d + HALF, d)
    theta = 2 * np.pi * row / ROWS
    phi = np.where(lane == LANES, np.pi, 2 * np.pi * (lane % LANES) / COLS)
    value = operators(theta, phi + 0 * theta)
    on_u, on_v, across = value.real.copy(), value.real.copy(), value.imag.copy()
    for at, angle in ((0, 0.0), (LANES, np.pi)):
        on_u[:, 0, 0, 0, at] = operators(np.array(0.0), np.array(angle)).real
        on_v[:, 0, 0, 0, at] = operators(np.array(np.pi), np.array(angle)).real
        across[:, 0, 0, 0, at] = 0.0
    table = np.concatenate([on_u, on_v, -across, across], axis=3)
    table = np.moveaxis(table, 0, 2)
    return table.reshape(2, GROUP, 16 * N_OPS, COLS).astype(np.float32)


def row_table():
    turns = slice_rows()[..., None] * np.arange(HALF) % ROWS
    angle = 2 * np.pi * turns / ROWS
    table = np.concatenate([np.cos(angle), np.sin(angle)], axis=2)
    return table.reshape(2, HALF, HALF).astype(np.float32)


def column_tables():
    c = np.arange(COLS)[:, None]
    n = np.arange(LANES)[None, :]
    angle = 2 * np.pi * ((c * n) % COLS) / COLS
    forward = np.concatenate([np.cos(angle), -np.sin(angle)], 1)
    forward[:, LANES] = np.where(np.arange(COLS) % 2 == 0, 1.0, -1.0)
    backward = 2.0 * forward.T / (ROWS * COLS)
    return forward.astype(np.float32), backward.astype(np.float32)


def dot(a, b):
    return jnp.dot(a, b, precision=HIGHEST, preferred_element_type=jnp.float32)


def halves(x):
    high = x.astype(jnp.bfloat16)
    return high, (x - high.astype(jnp.float32)).astype(jnp.bfloat16)


def dot_split(a, b):
    (ah, al), (bh, bl) = halves(a), halves(b)
    one = lambda x, y: jnp.dot(x, y, preferred_element_type=jnp.float32)
    return one(ah, bh) + (one(ah, bl) + one(al, bh))


def swap(x):
    return pltpu.roll(x, LANES, x.ndim - 1)


def flip(x):
    return pltpu.roll(x, QUAD, x.ndim - 2)


def tiles(x):
    return x.reshape(x.shape[0] // 8, 8, x.shape[1])


def iota(shape, dim):
    return lax.broadcasted_iota(jnp.int32, shape, dim)


def alternating(shape):
    return (1 - 2 * (iota(shape, 0) % 2)).astype(jnp.float32)


def parity():
    return (lax.axis_index("sp") + lax.axis_index("z1")) % 2


def prepare_kernel(src, init, rows, rows_t, table, src_o, init_o, rows_o, rows_t_o, table_o, sems):
    kind = parity()
    pairs = (
        (src, src_o),
        (rows.at[kind], rows_o),
        (init, init_o),
        (table.at[kind, own_slice()], table_o),
        (rows_t.at[kind], rows_t_o),
    )
    copies = [pltpu.make_async_copy(a, b, sems.at[n]) for n, (a, b) in enumerate(pairs)]
    for copy in copies:
        copy.start()
    for copy in copies:
        copy.wait()


def to_modes(product, first):
    a, b = tiles(product[:, :COLS]), tiles(product[:, COLS:])
    sub = iota(a.shape, 1)
    lane = iota(a.shape, 2)
    sign = jnp.where(sub < QUAD, 1.0, -1.0)
    own = sign * a
    b_flip = flip(b)
    result = jnp.where(lane < LANES, own + swap(flip(a)), swap(sign * b) + b_flip)
    edge = lane % LANES == 0
    zero_mode = jnp.logical_and(first, jnp.logical_and(iota(a.shape, 0) == 0, sub == QUAD))
    result = jnp.where(edge, jnp.where(zero_mode, b_flip, own), result)
    return result.reshape(product.shape[0], COLS)


def own_slice():
    return lax.axis_index("x") * 8 + lax.axis_index("z0") * 4 + lax.axis_index("y")


def fold(own, other):
    odd, lower = parity() == 1, lax.axis_index("sp") == 1
    own_sign = jnp.where(jnp.logical_and(odd, lower), -1.0, 1.0)
    other_sign = jnp.where(jnp.logical_and(odd, jnp.logical_not(lower)), -1.0, 1.0)
    return own_sign * own[...] + other_sign * other[...]


def columns(folded, col):
    y = dot(folded, col[...])
    return jnp.concatenate([y, y * alternating(y.shape)], axis=1)


def forward_kernel(src, src_other, col, rows, out):
    first = parity() == 0
    out[...] = to_modes(dot(rows[...], columns(fold(src, src_other), col)), first)


def initial_kernel(init, col, rows, out):
    at = own_slice()
    own_rows = rows[pl.ds(pl.multiple_of(8 * at, 8), 8), :]
    first = jnp.logical_and(parity() == 0, at == 0)
    part = to_modes(dot(own_rows, columns(init[...], col)), first)
    odd, lower = parity() == 1, lax.axis_index("sp") == 1
    out[...] = jnp.where(jnp.logical_and(odd, lower), -1.0, 1.0) * part


class Operators:
    def __init__(self, table):
        self.table = table

    def __call__(self, n, x):
        itself, partner = (self.table[16 * n + j : 16 * n + j + 8] for j in (0, 8))
        return itself * x + partner * flip(x)


def after(first, rest):
    return jnp.concatenate([first, rest], axis=1)


def place():
    return 2 * lax.axis_index("zh") + lax.axis_index("z1")


def scan_kernel(got, table, c_out, mean_out, message):
    op = Operators(table)
    f = got[...].reshape(4, RUN, 8, COLS)
    w = op(GUESS, f)
    t = w
    for level in range(3):
        d = 1 << level
        t = after(t[:, :d], t[:, d:] + op(COARSE + level, t[:, :-d]))
    c = after(w[:, :1], w[:, 1:] + op(DEFECT, t[:, :-1]))
    source_part = op(MEAN_SOURCE, f)
    c_out[...] = c
    mean_out[...] = after(source_part[:, :1], source_part[:, 1:] + op(MEAN_STATE, c[:, :-1]))
    message[0] = t[:, RUN - 1]
    message[1] = c[:, RUN - 1]


def join_kernel(own, other, init, table, message, kept):
    op = Operators(table)
    later = lax.axis_index("z1") == 1
    mine, theirs = own[0], other[0]
    prefix = jnp.where(later, theirs, 0.0)
    low = jnp.where(later, theirs, mine)
    high = jnp.where(later, mine, theirs)
    message[:4] = op(COARSE + 3, low) + high
    message[4:8] = own[1] + op(LAST_8, prefix)
    message[8] = init[...]
    kept[0] = prefix
    kept[1] = jnp.where(later, other[1], 0.0)


def finish_kernel(c_in, mean_in, kept, own, other, table, out):
    op = Operators(table)
    at = place()
    second = at >= 2
    at_start = at % 2 == 0
    mine, theirs, theirs_c = own[:4], other[:4], other[4:8]
    init = own[8] + other[8]
    low = jnp.where(second, theirs, mine)
    high = jnp.where(second, mine, theirs)
    total = op(COARSE + 4, low) + high
    state = [init]
    for x in range(3):
        state.append(op(COARSE + 5, state[x]) + total[x])
    state = jnp.stack(state)
    part = jnp.where(second, low, 0.0)
    part_c = jnp.where(second, theirs_c, 0.0)
    carry = kept[0] + jnp.where(at_start, part, op(COARSE + 3, part))
    before = kept[1] + jnp.where(at_start, part_c, op(LAST_8, part))
    by_8, by_16 = op(COARSE + 3, state), op(COARSE + 4, state)
    by_24 = op(COARSE + 3, by_16)
    carry = carry + jnp.where(
        at == 0, state, jnp.where(at == 1, by_8, jnp.where(at == 2, by_16, by_24))
    )
    to_last = jnp.where(at == 1, state, jnp.where(at == 2, by_8, by_16))
    before = before + op(LAST_8, to_last)
    ends = theirs_c[:3] + op(LAST_16, low[:3]) + op(LAST_32, state[:3])
    before = jnp.where(at == 0, jnp.concatenate([init[None], ends], axis=0), before)
    spread = carry[:, None]
    for level in range(3):
        spread = after(spread, op(COARSE + level, spread))
    added = op(DEFECT, spread)
    shift = after(before[:, None], added[:, :-1])
    c = c_in[...] + added
    mean = mean_in[...] + op(MEAN_STATE, shift)
    out[:, :8] = c.reshape(GROUP, 8, COLS)
    out[:, 8:] = mean.reshape(GROUP, 8, COLS)


def backward_kernel(got, rows_t, col, out, own_out):
    odd, lower = parity() == 1, lax.axis_index("sp") == 1
    got_v = got[...]
    parts = [got_v[:, :8], got_v[:, 8:]]
    shape = parts[0].shape
    sub = iota(shape, 1)
    origin = jnp.logical_and(iota(shape, 0) == 0, jnp.logical_and(sub == 0, iota(shape, 2) == 0))
    origin = jnp.logical_and(origin, jnp.logical_not(odd))
    constants = [jnp.where(odd, 0.0, v[0, :1, :1] * (1.0 / (ROWS * COLS))) for v in parts]
    parts = [jnp.where(origin, 0.0, v) for v in parts]
    flat = lambda v: v.reshape(HALF, COLS)
    left = [flat(jnp.where(sub < QUAD, v, -v)) for v in parts]
    right = [flat(flip(v)) for v in parts]
    product = dot_split(rows_t[...], jnp.concatenate(left + right, axis=1))
    sign = alternating((HALF, COLS))
    lane = iota((HALF, COLS), 1)
    own_sign = jnp.where(jnp.logical_and(odd, lower), -1.0, 1.0)
    sent_sign = jnp.where(jnp.logical_and(odd, jnp.logical_not(lower)), -1.0, 1.0)
    zero_mode = jnp.where(odd, 0.0, 0.5)
    for n, v in enumerate(parts):
        e = product[:, COLS * n : COLS * (n + 1)]
        f = product[:, COLS * (n + 2) : COLS * (n + 3)]
        y = jnp.where(lane < LANES, e + sign * swap(e), swap(f) + sign * f)
        first_u, first_v = v[0, :1], v[0, QUAD : QUAD + 1]
        edge = e + zero_mode * (sign * first_v - first_u)
        part = dot_split(jnp.where(lane % LANES == 0, edge, y), col[...]) + constants[n]
        out[n] = sent_sign * part
        own_out[n] = own_sign * part


PARAMS = pltpu.CompilerParams(vmem_limit_bytes=32 * 1024 * 1024)


def call(kernel, shapes, args, hbm=False, scratch=()):
    space = pltpu.HBM if hbm else pltpu.VMEM
    return pl.pallas_call(
        kernel,
        out_shape=[jax.ShapeDtypeStruct(s, jnp.float32) for s in shapes],
        in_specs=[pl.BlockSpec(memory_space=space)] * len(args),
        out_specs=[pl.BlockSpec(memory_space=pltpu.VMEM)] * len(shapes),
        scratch_shapes=scratch,
        compiler_params=PARAMS,
    )(*args)


def shards(initial, source):
    rows = row_table()
    forward, backward = column_tables()
    own = source[0]
    swap_two = [(0, 1), (1, 0)]
    src_other = lax.ppermute(own, "sp", swap_two)
    block = (HALF, COLS)
    square = (HALF, HALF)
    constants = [rows, rows.transpose(0, 2, 1).copy(), mode_table()]
    args = [own, initial, *(jnp.asarray(a) for a in constants)]
    src, init, rows_v, rows_t_v, table = call(
        prepare_kernel,
        [block, block, square, square, (16 * N_OPS, COLS)],
        [pltpu.with_memory_space_constraint(a, pltpu.HBM) for a in args],
        hbm=True,
        scratch=[pltpu.SemaphoreType.DMA((5,))],
    )
    (sent,) = call(forward_kernel, [block], [src, src_other, forward, rows_v])
    got = lax.all_to_all(sent.reshape(GROUP, 8, COLS), PLANE, 0, 0, tiled=True)
    runs, ends = (4, RUN, 8, COLS), (2, 4, 8, COLS)
    c, mean, message = call(scan_kernel, [runs, runs, ends], [got, table])
    init, message = lax.optimization_barrier((init, message))
    other = lax.ppermute(message, ("z1", "sp"), [(i, i ^ 3) for i in range(4)])
    (init_part,) = call(initial_kernel, [(8, COLS)], [init, forward, rows_v])
    message, kept = call(
        join_kernel, [(9, 8, COLS), ends], [message, other, init_part, table]
    )
    other = lax.ppermute(message, ("zh", "z1", "sp"), [(i, i ^ 7) for i in range(8)])
    (back,) = call(
        finish_kernel,
        [(GROUP, 16, COLS)],
        [c, mean, kept, message, other, table],
    )
    modes = lax.all_to_all(back, PLANE, 0, 0, tiled=True)
    part, own_part = call(
        backward_kernel, [(2, HALF, COLS), (2, HALF, COLS)], [modes, rows_t_v, backward]
    )
    other_part = lax.ppermute(part, "sp", swap_two)
    return own_part[:1] + other_part[:1], own_part[1:] + other_part[1:]


def solution(mesh):
    mesh = jax.sharding.Mesh(mesh.devices.reshape(MESH_SHAPE), MESH_AXES)
    by_block = P(MESH_AXES[:-1], "sp", None)
    return jax.shard_map(
        shards,
        mesh=mesh,
        in_specs=(P("sp", None), by_block),
        out_specs=(by_block, by_block),
        check_vma=False,
    )
```

```python
import jax
import jax.numpy as jnp
import ml_dtypes
import numpy as np
from jax import lax
from jax.experimental import pallas as pl
from jax.experimental.pallas import tpu as pltpu
from jax.sharding import PartitionSpec as P

ROWS = 512
HALF = ROWS // 2
COLS = 128
LANES = COLS // 2
STEPS = 16
GROUP = 32
QUAD = 4

fine_center = 0.2
fine_behind = 0.25
fine_ahead = 0.15
coarse_center = 0.04
coarse_behind = 0.31
coarse_ahead = 0.17

HIGHEST = lax.Precision.HIGHEST

MESH_SHAPE = (4, 2, 2, 2, 4, 2)
MESH_AXES = ("x", "zh", "z1", "z0", "y", "sp")
PLANE = ("x", "z0", "y")
RUN = 8

GUESS, DEFECT, MEAN_STATE, MEAN_SOURCE, COARSE = 0, 1, 2, 3, 4
LAST_8, LAST_16, LAST_32 = 10, 11, 12
N_OPS = 13


def symbol(theta, phi, center, behind, ahead):
    return (
        center
        + behind * np.exp(-1j * theta)
        + ahead * np.exp(1j * theta)
        + behind * np.exp(-1j * phi)
        + ahead * np.exp(1j * phi)
    )


def operators(theta, phi):
    fine = symbol(theta, phi, fine_center, fine_behind, fine_ahead)
    coarse = symbol(theta, phi, coarse_center, coarse_behind, coarse_ahead)
    power, total = np.ones_like(fine), np.zeros_like(fine)
    inner_sum = np.zeros_like(fine)
    inner_power = np.zeros_like(fine)
    for step in range(STEPS):
        total = total + power
        if step < STEPS - 1:
            inner_sum = inner_sum + total
        power = power * fine
        if step < STEPS - 1:
            inner_power = inner_power + power
    found = [total, power, inner_power / (STEPS - 1), inner_sum / (STEPS - 1)]
    found += [coarse ** (1 << n) for n in range(6)]
    found += [power * coarse ** (n - 1) for n in (8, 16, 32)]
    return np.stack(found)


def slice_rows():
    core = np.arange(2)[:, None, None]
    q = np.arange(GROUP)[None, :, None]
    return 2 * (QUAD * q + np.arange(QUAD)[None, None, :]) + core


def mode_table():
    d = slice_rows()[..., None]
    lane = np.arange(COLS)
    row = np.where(lane > LANES, d + HALF, d)
    theta = 2 * np.pi * row / ROWS
    phi = np.where(lane == LANES, np.pi, 2 * np.pi * (lane % LANES) / COLS)
    value = operators(theta, phi + 0 * theta)
    on_u, on_v, across = value.real.copy(), value.real.copy(), value.imag.copy()
    for at, angle in ((0, 0.0), (LANES, np.pi)):
        on_u[:, 0, 0, 0, at] = operators(np.array(0.0), np.array(angle)).real
        on_v[:, 0, 0, 0, at] = operators(np.array(np.pi), np.array(angle)).real
        across[:, 0, 0, 0, at] = 0.0
    table = np.concatenate([on_u, on_v, -across, across], axis=3)
    table = np.moveaxis(table, 0, 2)
    return table.reshape(2, GROUP, 16 * N_OPS, COLS).astype(np.float32)


def row_table():
    turns = slice_rows()[..., None] * np.arange(HALF) % ROWS
    angle = 2 * np.pi * turns / ROWS
    table = np.concatenate([np.cos(angle), np.sin(angle)], axis=2)
    return table.reshape(2, HALF, HALF)


def column_tables():
    c = np.arange(COLS)[:, None]
    n = np.arange(LANES)[None, :]
    angle = 2 * np.pi * ((c * n) % COLS) / COLS
    forward = np.concatenate([np.cos(angle), -np.sin(angle)], 1)
    forward[:, LANES] = np.where(np.arange(COLS) % 2 == 0, 1.0, -1.0)
    backward = 2.0 * forward.T / (ROWS * COLS)
    return forward, backward


def constant_terms(table, count):
    found, rest = [], table.astype(np.float64)
    for _ in range(count):
        found.append(rest.astype(ml_dtypes.bfloat16))
        rest = rest - found[-1].astype(np.float64)
    return found


def split_table(table, count):
    return np.concatenate(constant_terms(table, count), axis=-1)


def joined_table(table, pairs):
    found = constant_terms(table, 1 + max(j for _, j in pairs))
    return np.concatenate([found[j] for _, j in pairs], axis=0)


def dot(a, b):
    return jnp.dot(a, b, precision=HIGHEST, preferred_element_type=jnp.float32)


SIX = ((0, 0), (1, 0), (2, 0), (0, 1), (1, 1), (0, 2))
THREE = ((0, 0), (1, 0), (0, 1))


def terms(x, count):
    found = []
    for _ in range(count):
        found.append(x.astype(jnp.bfloat16))
        x = x - found[-1].astype(jnp.float32)
    return found


def joined(parts, order, axis):
    return jnp.concatenate([parts[n] for n in order], axis=axis)


def by_halves(left, right):
    half = left.shape[0] // 2
    rows = (left[:half], left[half:])
    return jnp.concatenate(
        [jnp.dot(part, right, preferred_element_type=jnp.float32) for part in rows], axis=0
    )


def times_table(x, table, pairs):
    left = joined(terms(x, 1 + max(i for i, _ in pairs)), [i for i, _ in pairs], 1)
    return by_halves(left, table)


def table_times(table, x, pairs):
    depth = x.shape[0]
    parts = [table[:, n * depth : (n + 1) * depth] for n in range(table.shape[1] // depth)]
    left = joined(parts, [j for _, j in pairs], 1)
    right = joined(terms(x, 1 + max(i for i, _ in pairs)), [i for i, _ in pairs], 0)
    return by_halves(left, right)


def swap(x):
    return pltpu.roll(x, LANES, x.ndim - 1)


def flip(x):
    return pltpu.roll(x, QUAD, x.ndim - 2)


def tiles(x):
    return x.reshape(x.shape[0] // 8, 8, x.shape[1])


def iota(shape, dim):
    return lax.broadcasted_iota(jnp.int32, shape, dim)


def alternating(shape):
    return (1 - 2 * (iota(shape, 0) % 2)).astype(jnp.float32)


def parity():
    return (lax.axis_index("sp") + lax.axis_index("z1")) % 2


def prepare_kernel(
    src, init, rows, rows_t, few, table, src_o, init_o, rows_o, rows_t_o, few_o, table_o, sems
):
    kind = parity()
    pairs = (
        (src, src_o),
        (rows.at[kind], rows_o),
        (init, init_o),
        (table.at[kind, own_slice()], table_o),
        (rows_t.at[kind], rows_t_o),
        (few.at[kind, own_slice()], few_o),
    )
    copies = [pltpu.make_async_copy(a, b, sems.at[n]) for n, (a, b) in enumerate(pairs)]
    for copy in copies:
        copy.start()
    for copy in copies:
        copy.wait()


def to_modes(product, first):
    a, b = tiles(product[:, :COLS]), tiles(product[:, COLS:])
    sub = iota(a.shape, 1)
    lane = iota(a.shape, 2)
    sign = jnp.where(sub < QUAD, 1.0, -1.0)
    own = sign * a
    b_flip = flip(b)
    result = jnp.where(lane < LANES, own + swap(flip(a)), swap(sign * b) + b_flip)
    edge = lane % LANES == 0
    zero_mode = jnp.logical_and(first, jnp.logical_and(iota(a.shape, 0) == 0, sub == QUAD))
    result = jnp.where(edge, jnp.where(zero_mode, b_flip, own), result)
    return result.reshape(product.shape[0], COLS)


def own_slice():
    return lax.axis_index("x") * 8 + lax.axis_index("z0") * 4 + lax.axis_index("y")


def fold(own, other):
    odd, lower = parity() == 1, lax.axis_index("sp") == 1
    own_sign = jnp.where(jnp.logical_and(odd, lower), -1.0, 1.0)
    other_sign = jnp.where(jnp.logical_and(odd, jnp.logical_not(lower)), -1.0, 1.0)
    return own_sign * own[...] + other_sign * other[...]


def columns(folded, col):
    y = times_table(folded, col[...], SIX)
    return jnp.concatenate([y, y * alternating(y.shape)], axis=1)


def forward_kernel(src, src_other, col, rows, out):
    first = parity() == 0
    product = table_times(rows[...], columns(fold(src, src_other), col), SIX)
    out[...] = to_modes(product, first)


def initial_kernel(init, col, rows, out):
    at = own_slice()
    first = jnp.logical_and(parity() == 0, at == 0)
    part = to_modes(dot(rows[...], columns(init[...], col)), first)
    odd, lower = parity() == 1, lax.axis_index("sp") == 1
    out[...] = jnp.where(jnp.logical_and(odd, lower), -1.0, 1.0) * part


class Operators:
    def __init__(self, table):
        self.table = table

    def __call__(self, n, x):
        itself, partner = (self.table[16 * n + j : 16 * n + j + 8] for j in (0, 8))
        return itself * x + partner * flip(x)


def after(first, rest):
    return jnp.concatenate([first, rest], axis=1)


def place():
    return 2 * lax.axis_index("zh") + lax.axis_index("z1")


def scan_kernel(got, table, c_out, mean_out, message):
    op = Operators(table)
    f = got[...].reshape(4, RUN, 8, COLS)
    w = op(GUESS, f)
    t = w
    for level in range(3):
        d = 1 << level
        t = after(t[:, :d], t[:, d:] + op(COARSE + level, t[:, :-d]))
    c = after(w[:, :1], w[:, 1:] + op(DEFECT, t[:, :-1]))
    source_part = op(MEAN_SOURCE, f)
    c_out[...] = c
    mean_out[...] = after(source_part[:, :1], source_part[:, 1:] + op(MEAN_STATE, c[:, :-1]))
    message[0] = t[:, RUN - 1]
    message[1] = c[:, RUN - 1]


def join_kernel(own, other, init, table, message, kept):
    op = Operators(table)
    later = lax.axis_index("z1") == 1
    mine, theirs = own[0], other[0]
    prefix = jnp.where(later, theirs, 0.0)
    low = jnp.where(later, theirs, mine)
    high = jnp.where(later, mine, theirs)
    message[:4] = op(COARSE + 3, low) + high
    message[4:8] = own[1] + op(LAST_8, prefix)
    message[8] = init[...]
    kept[0] = prefix
    kept[1] = jnp.where(later, other[1], 0.0)


def finish_kernel(c_in, mean_in, kept, own, other, table, out):
    op = Operators(table)
    at = place()
    second = at >= 2
    at_start = at % 2 == 0
    mine, theirs, theirs_c = own[:4], other[:4], other[4:8]
    init = own[8] + other[8]
    low = jnp.where(second, theirs, mine)
    high = jnp.where(second, mine, theirs)
    total = op(COARSE + 4, low) + high
    state = [init]
    for x in range(3):
        state.append(op(COARSE + 5, state[x]) + total[x])
    state = jnp.stack(state)
    part = jnp.where(second, low, 0.0)
    part_c = jnp.where(second, theirs_c, 0.0)
    carry = kept[0] + jnp.where(at_start, part, op(COARSE + 3, part))
    before = kept[1] + jnp.where(at_start, part_c, op(LAST_8, part))
    by_8, by_16 = op(COARSE + 3, state), op(COARSE + 4, state)
    by_24 = op(COARSE + 3, by_16)
    carry = carry + jnp.where(
        at == 0, state, jnp.where(at == 1, by_8, jnp.where(at == 2, by_16, by_24))
    )
    to_last = jnp.where(at == 1, state, jnp.where(at == 2, by_8, by_16))
    before = before + op(LAST_8, to_last)
    ends = theirs_c[:3] + op(LAST_16, low[:3]) + op(LAST_32, state[:3])
    before = jnp.where(at == 0, jnp.concatenate([init[None], ends], axis=0), before)
    spread = carry[:, None]
    for level in range(3):
        spread = after(spread, op(COARSE + level, spread))
    added = op(DEFECT, spread)
    shift = after(before[:, None], added[:, :-1])
    c = c_in[...] + added
    mean = mean_in[...] + op(MEAN_STATE, shift)
    out[:, :8] = c.reshape(GROUP, 8, COLS)
    out[:, 8:] = mean.reshape(GROUP, 8, COLS)


def backward_kernel(got, rows_t, col, out, own_out):
    odd, lower = parity() == 1, lax.axis_index("sp") == 1
    got_v = got[...]
    parts = [got_v[:, :8], got_v[:, 8:]]
    shape = parts[0].shape
    sub = iota(shape, 1)
    origin = jnp.logical_and(iota(shape, 0) == 0, jnp.logical_and(sub == 0, iota(shape, 2) == 0))
    origin = jnp.logical_and(origin, jnp.logical_not(odd))
    constants = [jnp.where(odd, 0.0, v[0, :1, :1] * (1.0 / (ROWS * COLS))) for v in parts]
    parts = [jnp.where(origin, 0.0, v) for v in parts]
    flat = lambda v: v.reshape(HALF, COLS)
    left = [flat(jnp.where(sub < QUAD, v, -v)) for v in parts]
    right = [flat(flip(v)) for v in parts]
    product = table_times(rows_t[...], jnp.concatenate(left + right, axis=1), THREE)
    sign = alternating((HALF, COLS))
    lane = iota((HALF, COLS), 1)
    own_sign = jnp.where(jnp.logical_and(odd, lower), -1.0, 1.0)
    sent_sign = jnp.where(jnp.logical_and(odd, jnp.logical_not(lower)), -1.0, 1.0)
    zero_mode = jnp.where(odd, 0.0, 0.5)
    for n, v in enumerate(parts):
        e = product[:, COLS * n : COLS * (n + 1)]
        f = product[:, COLS * (n + 2) : COLS * (n + 3)]
        y = jnp.where(lane < LANES, e + sign * swap(e), swap(f) + sign * f)
        first_u, first_v = v[0, :1], v[0, QUAD : QUAD + 1]
        edge = e + zero_mode * (sign * first_v - first_u)
        y = jnp.where(lane % LANES == 0, edge, y)
        part = times_table(y, col[...], THREE) + constants[n]
        out[n] = sent_sign * part
        own_out[n] = own_sign * part


PARAMS = pltpu.CompilerParams(vmem_limit_bytes=32 * 1024 * 1024)


def call(kernel, shapes, args, hbm=False, scratch=()):
    space = pltpu.HBM if hbm else pltpu.VMEM
    return pl.pallas_call(
        kernel,
        out_shape=[
            jax.ShapeDtypeStruct(s, jnp.float32) if isinstance(s, tuple) else s for s in shapes
        ],
        in_specs=[pl.BlockSpec(memory_space=space)] * len(args),
        out_specs=[pl.BlockSpec(memory_space=pltpu.VMEM)] * len(shapes),
        scratch_shapes=scratch,
        compiler_params=PARAMS,
    )(*args)


def shards(initial, source):
    rows = row_table()
    forward, backward = column_tables()
    forward, backward = joined_table(forward, SIX), joined_table(backward, THREE)
    rows_split = split_table(rows, 3)
    rows_t_split = split_table(rows.transpose(0, 2, 1), 2)
    few_rows = rows.reshape(2, GROUP, 8, HALF).astype(np.float32)
    own = source[0]
    swap_two = [(0, 1), (1, 0)]
    src_other = lax.ppermute(own, "sp", swap_two)
    block = (HALF, COLS)
    constants = [rows_split, rows_t_split, few_rows, mode_table()]
    args = [own, initial, *(jnp.asarray(a) for a in constants)]
    bf16 = jnp.bfloat16
    src, init, rows_v, rows_t_v, few, table = call(
        prepare_kernel,
        [
            block,
            block,
            jax.ShapeDtypeStruct((HALF, 3 * HALF), bf16),
            jax.ShapeDtypeStruct((HALF, 2 * HALF), bf16),
            (8, HALF),
            (16 * N_OPS, COLS),
        ],
        [pltpu.with_memory_space_constraint(a, pltpu.HBM) for a in args],
        hbm=True,
        scratch=[pltpu.SemaphoreType.DMA((6,))],
    )
    (sent,) = call(forward_kernel, [block], [src, src_other, forward, rows_v])
    got = lax.all_to_all(sent.reshape(GROUP, 8, COLS), PLANE, 0, 0, tiled=True)
    runs, ends = (4, RUN, 8, COLS), (2, 4, 8, COLS)
    c, mean, message = call(scan_kernel, [runs, runs, ends], [got, table])
    init, message = lax.optimization_barrier((init, message))
    other = lax.ppermute(message, ("z1", "sp"), [(i, i ^ 3) for i in range(4)])
    (init_part,) = call(initial_kernel, [(8, COLS)], [init, forward, few])
    message, kept = call(
        join_kernel, [(9, 8, COLS), ends], [message, other, init_part, table]
    )
    other = lax.ppermute(message, ("zh", "z1", "sp"), [(i, i ^ 7) for i in range(8)])
    (back,) = call(
        finish_kernel,
        [(GROUP, 16, COLS)],
        [c, mean, kept, message, other, table],
    )
    modes = lax.all_to_all(back, PLANE, 0, 0, tiled=True)
    part, own_part = call(
        backward_kernel, [(2, HALF, COLS), (2, HALF, COLS)], [modes, rows_t_v, backward]
    )
    other_part = lax.ppermute(part, "sp", swap_two)
    return own_part[:1] + other_part[:1], own_part[1:] + other_part[1:]


def solution(mesh):
    mesh = jax.sharding.Mesh(mesh.devices.reshape(MESH_SHAPE), MESH_AXES)
    by_block = P(MESH_AXES[:-1], "sp", None)
    return jax.shard_map(
        shards,
        mesh=mesh,
        in_specs=(P("sp", None), by_block),
        out_specs=(by_block, by_block),
        check_vma=False,
    )
```

```python
import jax
import jax.numpy as jnp
import ml_dtypes
import numpy as np
from jax import lax
from jax.experimental import pallas as pl
from jax.experimental.pallas import tpu as pltpu
from jax.sharding import PartitionSpec as P

ROWS = 512
HALF = ROWS // 2
COLS = 128
LANES = COLS // 2
STEPS = 16
GROUP = 32
QUAD = 4

fine_center = 0.2
fine_behind = 0.25
fine_ahead = 0.15
coarse_center = 0.04
coarse_behind = 0.31
coarse_ahead = 0.17

HIGHEST = lax.Precision.HIGHEST

MESH_SHAPE = (4, 2, 2, 2, 4, 2)
MESH_AXES = ("x", "zh", "z1", "z0", "y", "sp")
PLANE = ("x", "z0", "y")
RUN = 8

GUESS, DEFECT, MEAN_STATE, MEAN_SOURCE, COARSE = 0, 1, 2, 3, 4
LAST_8, LAST_16, LAST_32 = 10, 11, 12
N_OPS = 13


def symbol(theta, phi, center, behind, ahead):
    return (
        center
        + behind * np.exp(-1j * theta)
        + ahead * np.exp(1j * theta)
        + behind * np.exp(-1j * phi)
        + ahead * np.exp(1j * phi)
    )


def operators(theta, phi):
    fine = symbol(theta, phi, fine_center, fine_behind, fine_ahead)
    coarse = symbol(theta, phi, coarse_center, coarse_behind, coarse_ahead)
    power, total = np.ones_like(fine), np.zeros_like(fine)
    inner_sum = np.zeros_like(fine)
    inner_power = np.zeros_like(fine)
    for step in range(STEPS):
        total = total + power
        if step < STEPS - 1:
            inner_sum = inner_sum + total
        power = power * fine
        if step < STEPS - 1:
            inner_power = inner_power + power
    found = [total, power, inner_power / (STEPS - 1), inner_sum / (STEPS - 1)]
    found += [coarse ** (1 << n) for n in range(6)]
    found += [power * coarse ** (n - 1) for n in (8, 16, 32)]
    return np.stack(found)


def slice_rows():
    core = np.arange(2)[:, None, None]
    q = np.arange(GROUP)[None, :, None]
    return 2 * (QUAD * q + np.arange(QUAD)[None, None, :]) + core


def mode_table():
    d = slice_rows()[..., None]
    lane = np.arange(COLS)
    row = np.where(lane > LANES, d + HALF, d)
    theta = 2 * np.pi * row / ROWS
    phi = np.where(lane == LANES, np.pi, 2 * np.pi * (lane % LANES) / COLS)
    value = operators(theta, phi + 0 * theta)
    on_u, on_v, across = value.real.copy(), value.real.copy(), value.imag.copy()
    for at, angle in ((0, 0.0), (LANES, np.pi)):
        on_u[:, 0, 0, 0, at] = operators(np.array(0.0), np.array(angle)).real
        on_v[:, 0, 0, 0, at] = operators(np.array(np.pi), np.array(angle)).real
        across[:, 0, 0, 0, at] = 0.0
    table = np.concatenate([on_u, on_v, -across, across], axis=3)
    table = np.moveaxis(table, 0, 2)
    return table.reshape(2, GROUP, 16 * N_OPS, COLS).astype(np.float32)


def row_table():
    turns = slice_rows()[..., None] * np.arange(HALF) % ROWS
    angle = 2 * np.pi * turns / ROWS
    table = np.concatenate([np.cos(angle), np.sin(angle)], axis=2)
    return table.reshape(2, HALF, HALF)


def column_tables():
    c = np.arange(COLS)[:, None]
    n = np.arange(LANES)[None, :]
    angle = 2 * np.pi * ((c * n) % COLS) / COLS
    forward = np.concatenate([np.cos(angle), -np.sin(angle)], 1)
    forward[:, LANES] = np.where(np.arange(COLS) % 2 == 0, 1.0, -1.0)
    backward = 2.0 * forward.T / (ROWS * COLS)
    return forward, backward


def constant_terms(table, count):
    found, rest = [], table.astype(np.float64)
    for _ in range(count):
        found.append(rest.astype(ml_dtypes.bfloat16))
        rest = rest - found[-1].astype(np.float64)
    return found


def split_table(table, count):
    return np.concatenate(constant_terms(table, count), axis=-1)


def joined_table(table, pairs):
    found = constant_terms(table, 1 + max(j for _, j in pairs))
    return np.concatenate([found[j] for _, j in pairs], axis=0)


def dot(a, b):
    return jnp.dot(a, b, precision=HIGHEST, preferred_element_type=jnp.float32)


SIX = ((0, 0), (1, 0), (2, 0), (0, 1), (1, 1), (0, 2))
THREE = ((0, 0), (1, 0), (0, 1))


def terms(x, count):
    found = []
    for _ in range(count):
        found.append(x.astype(jnp.bfloat16))
        x = x - found[-1].astype(jnp.float32)
    return found


def joined(parts, order, axis):
    return jnp.concatenate([parts[n] for n in order], axis=axis)


def by_halves(left, right):
    half = left.shape[0] // 2
    rows = (left[:half], left[half:])
    return jnp.concatenate(
        [jnp.dot(part, right, preferred_element_type=jnp.float32) for part in rows], axis=0
    )


def times_table(x, table, pairs):
    left = joined(terms(x, 1 + max(i for i, _ in pairs)), [i for i, _ in pairs], 1)
    return by_halves(left, table)


def table_times(table, x, pairs):
    depth = x.shape[0]
    parts = [table[:, n * depth : (n + 1) * depth] for n in range(table.shape[1] // depth)]
    left = joined(parts, [j for _, j in pairs], 1)
    right = joined(terms(x, 1 + max(i for i, _ in pairs)), [i for i, _ in pairs], 0)
    if len(pairs) % 2:
        return by_halves(left, right)
    cut = left.shape[1] // 2
    near = jnp.dot(left[:, :cut], right[:cut], preferred_element_type=jnp.float32)
    return near + jnp.dot(left[:, cut:], right[cut:], preferred_element_type=jnp.float32)


def swap(x):
    return pltpu.roll(x, LANES, x.ndim - 1)


def flip(x):
    return pltpu.roll(x, QUAD, x.ndim - 2)


def tiles(x):
    return x.reshape(x.shape[0] // 8, 8, x.shape[1])


def iota(shape, dim):
    return lax.broadcasted_iota(jnp.int32, shape, dim)


def alternating(shape):
    return (1 - 2 * (iota(shape, 0) % 2)).astype(jnp.float32)


def parity():
    return (lax.axis_index("sp") + lax.axis_index("z1")) % 2


def prepare_kernel(
    src, init, rows, rows_t, few, table, src_o, init_o, rows_o, rows_t_o, few_o, table_o, sems
):
    kind = parity()
    pairs = (
        (src, src_o),
        (rows.at[kind], rows_o),
        (init, init_o),
        (table.at[kind, own_slice()], table_o),
        (rows_t.at[kind], rows_t_o),
        (few.at[kind, own_slice()], few_o),
    )
    copies = [pltpu.make_async_copy(a, b, sems.at[n]) for n, (a, b) in enumerate(pairs)]
    for copy in copies:
        copy.start()
    for copy in copies:
        copy.wait()


def to_modes(product, first):
    a, b = tiles(product[:, :COLS]), tiles(product[:, COLS:])
    sub = iota(a.shape, 1)
    lane = iota(a.shape, 2)
    sign = jnp.where(sub < QUAD, 1.0, -1.0)
    own = sign * a
    b_flip = flip(b)
    result = jnp.where(lane < LANES, own + swap(flip(a)), swap(sign * b) + b_flip)
    edge = lane % LANES == 0
    zero_mode = jnp.logical_and(first, jnp.logical_and(iota(a.shape, 0) == 0, sub == QUAD))
    result = jnp.where(edge, jnp.where(zero_mode, b_flip, own), result)
    return result.reshape(product.shape[0], COLS)


def own_slice():
    return lax.axis_index("x") * 8 + lax.axis_index("z0") * 4 + lax.axis_index("y")


def fold(own, other):
    odd, lower = parity() == 1, lax.axis_index("sp") == 1
    own_sign = jnp.where(jnp.logical_and(odd, lower), -1.0, 1.0)
    other_sign = jnp.where(jnp.logical_and(odd, jnp.logical_not(lower)), -1.0, 1.0)
    return own_sign * own[...] + other_sign * other[...]


def columns(folded, col):
    y = times_table(folded, col[...], SIX)
    return jnp.concatenate([y, y * alternating(y.shape)], axis=1)


def forward_kernel(src, src_other, col, rows, out):
    first = parity() == 0
    product = table_times(rows[...], columns(fold(src, src_other), col), SIX)
    out[...] = to_modes(product, first)


def initial_kernel(init, col, rows, out):
    at = own_slice()
    first = jnp.logical_and(parity() == 0, at == 0)
    part = to_modes(dot(rows[...], columns(init[...], col)), first)
    odd, lower = parity() == 1, lax.axis_index("sp") == 1
    out[...] = jnp.where(jnp.logical_and(odd, lower), -1.0, 1.0) * part


class Operators:
    def __init__(self, table):
        self.table = table

    def __call__(self, n, x):
        itself, partner = (self.table[16 * n + j : 16 * n + j + 8] for j in (0, 8))
        return itself * x + partner * flip(x)


def after(first, rest):
    return jnp.concatenate([first, rest], axis=1)


def place():
    return 2 * lax.axis_index("zh") + lax.axis_index("z1")


def scan_kernel(got, table, c_out, mean_out, message):
    op = Operators(table)
    f = got[...].reshape(4, RUN, 8, COLS)
    w = op(GUESS, f)
    t = w
    for level in range(3):
        d = 1 << level
        t = after(t[:, :d], t[:, d:] + op(COARSE + level, t[:, :-d]))
    c = after(w[:, :1], w[:, 1:] + op(DEFECT, t[:, :-1]))
    source_part = op(MEAN_SOURCE, f)
    c_out[...] = c
    mean_out[...] = after(source_part[:, :1], source_part[:, 1:] + op(MEAN_STATE, c[:, :-1]))
    message[0] = t[:, RUN - 1]
    message[1] = c[:, RUN - 1]


def join_kernel(own, other, init, table, message, kept):
    op = Operators(table)
    later = lax.axis_index("z1") == 1
    mine, theirs = own[0], other[0]
    prefix = jnp.where(later, theirs, 0.0)
    low = jnp.where(later, theirs, mine)
    high = jnp.where(later, mine, theirs)
    message[:4] = op(COARSE + 3, low) + high
    message[4:8] = own[1] + op(LAST_8, prefix)
    message[8] = init[...]
    kept[0] = prefix
    kept[1] = jnp.where(later, other[1], 0.0)


def finish_kernel(c_in, mean_in, kept, own, other, table, out):
    op = Operators(table)
    at = place()
    second = at >= 2
    at_start = at % 2 == 0
    mine, theirs, theirs_c = own[:4], other[:4], other[4:8]
    init = own[8] + other[8]
    low = jnp.where(second, theirs, mine)
    high = jnp.where(second, mine, theirs)
    total = op(COARSE + 4, low) + high
    state = [init]
    for x in range(3):
        state.append(op(COARSE + 5, state[x]) + total[x])
    state = jnp.stack(state)
    part = jnp.where(second, low, 0.0)
    part_c = jnp.where(second, theirs_c, 0.0)
    carry = kept[0] + jnp.where(at_start, part, op(COARSE + 3, part))
    before = kept[1] + jnp.where(at_start, part_c, op(LAST_8, part))
    by_8, by_16 = op(COARSE + 3, state), op(COARSE + 4, state)
    by_24 = op(COARSE + 3, by_16)
    carry = carry + jnp.where(
        at == 0, state, jnp.where(at == 1, by_8, jnp.where(at == 2, by_16, by_24))
    )
    to_last = jnp.where(at == 1, state, jnp.where(at == 2, by_8, by_16))
    before = before + op(LAST_8, to_last)
    ends = theirs_c[:3] + op(LAST_16, low[:3]) + op(LAST_32, state[:3])
    before = jnp.where(at == 0, jnp.concatenate([init[None], ends], axis=0), before)
    spread = carry[:, None]
    for level in range(3):
        spread = after(spread, op(COARSE + level, spread))
    added = op(DEFECT, spread)
    shift = after(before[:, None], added[:, :-1])
    c = c_in[...] + added
    mean = mean_in[...] + op(MEAN_STATE, shift)
    out[:, :8] = c.reshape(GROUP, 8, COLS)
    out[:, 8:] = mean.reshape(GROUP, 8, COLS)


def backward_kernel(got, rows_t, col, out, own_out):
    odd, lower = parity() == 1, lax.axis_index("sp") == 1
    got_v = got[...]
    parts = [got_v[:, :8], got_v[:, 8:]]
    shape = parts[0].shape
    sub = iota(shape, 1)
    origin = jnp.logical_and(iota(shape, 0) == 0, jnp.logical_and(sub == 0, iota(shape, 2) == 0))
    origin = jnp.logical_and(origin, jnp.logical_not(odd))
    constants = [jnp.where(odd, 0.0, v[0, :1, :1] * (1.0 / (ROWS * COLS))) for v in parts]
    parts = [jnp.where(origin, 0.0, v) for v in parts]
    flat = lambda v: v.reshape(HALF, COLS)
    left = [flat(jnp.where(sub < QUAD, v, -v)) for v in parts]
    right = [flat(flip(v)) for v in parts]
    product = table_times(rows_t[...], jnp.concatenate(left + right, axis=1), THREE)
    sign = alternating((HALF, COLS))
    lane = iota((HALF, COLS), 1)
    own_sign = jnp.where(jnp.logical_and(odd, lower), -1.0, 1.0)
    sent_sign = jnp.where(jnp.logical_and(odd, jnp.logical_not(lower)), -1.0, 1.0)
    zero_mode = jnp.where(odd, 0.0, 0.5)
    for n, v in enumerate(parts):
        e = product[:, COLS * n : COLS * (n + 1)]
        f = product[:, COLS * (n + 2) : COLS * (n + 3)]
        y = jnp.where(lane < LANES, e + sign * swap(e), swap(f) + sign * f)
        first_u, first_v = v[0, :1], v[0, QUAD : QUAD + 1]
        edge = e + zero_mode * (sign * first_v - first_u)
        y = jnp.where(lane % LANES == 0, edge, y)
        part = times_table(y, col[...], THREE) + constants[n]
        out[n] = sent_sign * part
        own_out[n] = own_sign * part


PARAMS = pltpu.CompilerParams(vmem_limit_bytes=32 * 1024 * 1024)


def call(kernel, shapes, args, hbm=False, scratch=()):
    space = pltpu.HBM if hbm else pltpu.VMEM
    return pl.pallas_call(
        kernel,
        out_shape=[
            jax.ShapeDtypeStruct(s, jnp.float32) if isinstance(s, tuple) else s for s in shapes
        ],
        in_specs=[pl.BlockSpec(memory_space=space)] * len(args),
        out_specs=[pl.BlockSpec(memory_space=pltpu.VMEM)] * len(shapes),
        scratch_shapes=scratch,
        compiler_params=PARAMS,
    )(*args)


def shards(initial, source):
    rows = row_table()
    forward, backward = column_tables()
    forward, backward = joined_table(forward, SIX), joined_table(backward, THREE)
    rows_split = split_table(rows, 3)
    rows_t_split = split_table(rows.transpose(0, 2, 1), 2)
    few_rows = rows.reshape(2, GROUP, 8, HALF).astype(np.float32)
    own = source[0]
    swap_two = [(0, 1), (1, 0)]
    src_other = lax.ppermute(own, "sp", swap_two)
    block = (HALF, COLS)
    constants = [rows_split, rows_t_split, few_rows, mode_table()]
    args = [own, initial, *(jnp.asarray(a) for a in constants)]
    bf16 = jnp.bfloat16
    src, init, rows_v, rows_t_v, few, table = call(
        prepare_kernel,
        [
            block,
            block,
            jax.ShapeDtypeStruct((HALF, 3 * HALF), bf16),
            jax.ShapeDtypeStruct((HALF, 2 * HALF), bf16),
            (8, HALF),
            (16 * N_OPS, COLS),
        ],
        [pltpu.with_memory_space_constraint(a, pltpu.HBM) for a in args],
        hbm=True,
        scratch=[pltpu.SemaphoreType.DMA((6,))],
    )
    (sent,) = call(forward_kernel, [block], [src, src_other, forward, rows_v])
    got = lax.all_to_all(sent.reshape(GROUP, 8, COLS), PLANE, 0, 0, tiled=True)
    runs, ends = (4, RUN, 8, COLS), (2, 4, 8, COLS)
    c, mean, message = call(scan_kernel, [runs, runs, ends], [got, table])
    init, message = lax.optimization_barrier((init, message))
    other = lax.ppermute(message, ("z1", "sp"), [(i, i ^ 3) for i in range(4)])
    (init_part,) = call(initial_kernel, [(8, COLS)], [init, forward, few])
    message, kept = call(
        join_kernel, [(9, 8, COLS), ends], [message, other, init_part, table]
    )
    other = lax.ppermute(message, ("zh", "z1", "sp"), [(i, i ^ 7) for i in range(8)])
    (back,) = call(
        finish_kernel,
        [(GROUP, 16, COLS)],
        [c, mean, kept, message, other, table],
    )
    modes = lax.all_to_all(back, PLANE, 0, 0, tiled=True)
    part, own_part = call(
        backward_kernel, [(2, HALF, COLS), (2, HALF, COLS)], [modes, rows_t_v, backward]
    )
    other_part = lax.ppermute(part, "sp", swap_two)
    return own_part[:1] + other_part[:1], own_part[1:] + other_part[1:]


def solution(mesh):
    mesh = jax.sharding.Mesh(mesh.devices.reshape(MESH_SHAPE), MESH_AXES)
    by_block = P(MESH_AXES[:-1], "sp", None)
    return jax.shard_map(
        shards,
        mesh=mesh,
        in_specs=(P("sp", None), by_block),
        out_specs=(by_block, by_block),
        check_vma=False,
    )
```

```python
import jax
import jax.numpy as jnp
import ml_dtypes
import numpy as np
from jax import lax
from jax.experimental import pallas as pl
from jax.experimental.pallas import tpu as pltpu
from jax.sharding import PartitionSpec as P

ROWS = 512
HALF = ROWS // 2
COLS = 128
LANES = COLS // 2
STEPS = 16
GROUP = 32
QUAD = 4

fine_center = 0.2
fine_behind = 0.25
fine_ahead = 0.15
coarse_center = 0.04
coarse_behind = 0.31
coarse_ahead = 0.17

HIGHEST = lax.Precision.HIGHEST

MESH_SHAPE = (4, 2, 2, 2, 4, 2)
MESH_AXES = ("x", "zh", "z1", "z0", "y", "sp")
PLANE = ("x", "z0", "y")
RUN = 8

GUESS, DEFECT, MEAN_STATE, MEAN_SOURCE, COARSE = 0, 1, 2, 3, 4
LAST_8, LAST_16, LAST_32 = 10, 11, 12
N_OPS = 13


def symbol(theta, phi, center, behind, ahead):
    return (
        center
        + behind * np.exp(-1j * theta)
        + ahead * np.exp(1j * theta)
        + behind * np.exp(-1j * phi)
        + ahead * np.exp(1j * phi)
    )


def operators(theta, phi):
    fine = symbol(theta, phi, fine_center, fine_behind, fine_ahead)
    coarse = symbol(theta, phi, coarse_center, coarse_behind, coarse_ahead)
    power, total = np.ones_like(fine), np.zeros_like(fine)
    inner_sum = np.zeros_like(fine)
    inner_power = np.zeros_like(fine)
    for step in range(STEPS):
        total = total + power
        if step < STEPS - 1:
            inner_sum = inner_sum + total
        power = power * fine
        if step < STEPS - 1:
            inner_power = inner_power + power
    found = [total, power, inner_power / (STEPS - 1), inner_sum / (STEPS - 1)]
    found += [coarse ** (1 << n) for n in range(6)]
    found += [power * coarse ** (n - 1) for n in (8, 16, 32)]
    return np.stack(found)


def slice_rows():
    core = np.arange(2)[:, None, None]
    q = np.arange(GROUP)[None, :, None]
    return 2 * (QUAD * q + np.arange(QUAD)[None, None, :]) + core


def mode_table():
    d = slice_rows()[..., None]
    lane = np.arange(COLS)
    row = np.where(lane > LANES, d + HALF, d)
    theta = 2 * np.pi * row / ROWS
    phi = np.where(lane == LANES, np.pi, 2 * np.pi * (lane % LANES) / COLS)
    value = operators(theta, phi + 0 * theta)
    on_u, on_v, across = value.real.copy(), value.real.copy(), value.imag.copy()
    for at, angle in ((0, 0.0), (LANES, np.pi)):
        on_u[:, 0, 0, 0, at] = operators(np.array(0.0), np.array(angle)).real
        on_v[:, 0, 0, 0, at] = operators(np.array(np.pi), np.array(angle)).real
        across[:, 0, 0, 0, at] = 0.0
    table = np.concatenate([on_u, on_v, -across, across], axis=3)
    table = np.moveaxis(table, 0, 2)
    return table.reshape(2, GROUP, 16 * N_OPS, COLS).astype(np.float32)


def row_table():
    turns = slice_rows()[..., None] * np.arange(HALF) % ROWS
    angle = 2 * np.pi * turns / ROWS
    table = np.concatenate([np.cos(angle), np.sin(angle)], axis=2)
    return table.reshape(2, HALF, HALF)


def column_tables():
    c = np.arange(COLS)[:, None]
    n = np.arange(LANES)[None, :]
    angle = 2 * np.pi * ((c * n) % COLS) / COLS
    forward = np.concatenate([np.cos(angle), -np.sin(angle)], 1)
    forward[:, LANES] = np.where(np.arange(COLS) % 2 == 0, 1.0, -1.0)
    backward = 2.0 * forward.T / (ROWS * COLS)
    return forward, backward


def constant_terms(table, count):
    found, rest = [], table.astype(np.float64)
    for _ in range(count):
        found.append(rest.astype(ml_dtypes.bfloat16))
        rest = rest - found[-1].astype(np.float64)
    return found


def split_table(table, count):
    return np.concatenate(constant_terms(table, count), axis=-1)


def joined_table(table, pairs):
    found = constant_terms(table, 1 + max(j for _, j in pairs))
    return np.concatenate([found[j] for _, j in pairs], axis=0)


def dot(a, b):
    return jnp.dot(a, b, precision=HIGHEST, preferred_element_type=jnp.float32)


SIX = ((0, 0), (1, 0), (2, 0), (0, 1), (1, 1), (0, 2))
THREE = ((0, 0), (1, 0), (0, 1))


def terms(x, count):
    found = []
    for _ in range(count):
        found.append(x.astype(jnp.bfloat16))
        x = x - found[-1].astype(jnp.float32)
    return found


def joined(parts, order, axis):
    return jnp.concatenate([parts[n] for n in order], axis=axis)


def by_halves(left, right):
    half = left.shape[0] // 2
    rows = (left[:half], left[half:])
    return jnp.concatenate(
        [jnp.dot(part, right, preferred_element_type=jnp.float32) for part in rows], axis=0
    )


def times_table(x, table, pairs):
    left = joined(terms(x, 1 + max(i for i, _ in pairs)), [i for i, _ in pairs], 1)
    if len(pairs) % 2:
        return by_halves(left, table)
    cut = 2 * left.shape[1] // 3
    near = jnp.dot(left[:, :cut], table[:cut], preferred_element_type=jnp.float32)
    return near + jnp.dot(left[:, cut:], table[cut:], preferred_element_type=jnp.float32)


def table_times(table, x, pairs):
    depth = x.shape[0]
    parts = [table[:, n * depth : (n + 1) * depth] for n in range(table.shape[1] // depth)]
    left = joined(parts, [j for _, j in pairs], 1)
    right = joined(terms(x, 1 + max(i for i, _ in pairs)), [i for i, _ in pairs], 0)
    if len(pairs) % 2:
        return by_halves(left, right)
    cut = left.shape[1] // 2
    near = jnp.dot(left[:, :cut], right[:cut], preferred_element_type=jnp.float32)
    return near + jnp.dot(left[:, cut:], right[cut:], preferred_element_type=jnp.float32)


def swap(x):
    return pltpu.roll(x, LANES, x.ndim - 1)


def flip(x):
    return pltpu.roll(x, QUAD, x.ndim - 2)


def tiles(x):
    return x.reshape(x.shape[0] // 8, 8, x.shape[1])


def iota(shape, dim):
    return lax.broadcasted_iota(jnp.int32, shape, dim)


def alternating(shape):
    return (1 - 2 * (iota(shape, 0) % 2)).astype(jnp.float32)


def parity():
    return (lax.axis_index("sp") + lax.axis_index("z1")) % 2


def prepare_kernel(
    src, init, rows, rows_t, few, table, src_o, init_o, rows_o, rows_t_o, few_o, table_o, sems
):
    kind = parity()
    pairs = (
        (src, src_o),
        (rows.at[kind], rows_o),
        (init, init_o),
        (table.at[kind, own_slice()], table_o),
        (rows_t.at[kind], rows_t_o),
        (few.at[kind, own_slice()], few_o),
    )
    copies = [pltpu.make_async_copy(a, b, sems.at[n]) for n, (a, b) in enumerate(pairs)]
    for copy in copies:
        copy.start()
    for copy in copies:
        copy.wait()


def to_modes(product, first):
    a, b = tiles(product[:, :COLS]), tiles(product[:, COLS:])
    sub = iota(a.shape, 1)
    lane = iota(a.shape, 2)
    sign = jnp.where(sub < QUAD, 1.0, -1.0)
    own = sign * a
    b_flip = flip(b)
    result = jnp.where(lane < LANES, own + swap(flip(a)), swap(sign * b) + b_flip)
    edge = lane % LANES == 0
    zero_mode = jnp.logical_and(first, jnp.logical_and(iota(a.shape, 0) == 0, sub == QUAD))
    result = jnp.where(edge, jnp.where(zero_mode, b_flip, own), result)
    return result.reshape(product.shape[0], COLS)


def own_slice():
    return lax.axis_index("x") * 8 + lax.axis_index("z0") * 4 + lax.axis_index("y")


def fold(own, other):
    odd, lower = parity() == 1, lax.axis_index("sp") == 1
    own_sign = jnp.where(jnp.logical_and(odd, lower), -1.0, 1.0)
    other_sign = jnp.where(jnp.logical_and(odd, jnp.logical_not(lower)), -1.0, 1.0)
    return own_sign * own[...] + other_sign * other[...]


def columns(folded, col):
    y = times_table(folded, col[...], SIX)
    return jnp.concatenate([y, y * alternating(y.shape)], axis=1)


def forward_kernel(src, src_other, col, rows, out):
    first = parity() == 0
    product = table_times(rows[...], columns(fold(src, src_other), col), SIX)
    out[...] = to_modes(product, first)


def initial_kernel(init, col, rows, out):
    at = own_slice()
    first = jnp.logical_and(parity() == 0, at == 0)
    part = to_modes(dot(rows[...], columns(init[...], col)), first)
    odd, lower = parity() == 1, lax.axis_index("sp") == 1
    out[...] = jnp.where(jnp.logical_and(odd, lower), -1.0, 1.0) * part


class Operators:
    def __init__(self, table):
        self.table = table

    def __call__(self, n, x):
        itself, partner = (self.table[16 * n + j : 16 * n + j + 8] for j in (0, 8))
        return itself * x + partner * flip(x)


def after(first, rest):
    return jnp.concatenate([first, rest], axis=1)


def place():
    return 2 * lax.axis_index("zh") + lax.axis_index("z1")


def scan_kernel(got, table, c_out, mean_out, message):
    op = Operators(table)
    f = got[...].reshape(4, RUN, 8, COLS)
    w = op(GUESS, f)
    t = w
    for level in range(3):
        d = 1 << level
        t = after(t[:, :d], t[:, d:] + op(COARSE + level, t[:, :-d]))
    c = after(w[:, :1], w[:, 1:] + op(DEFECT, t[:, :-1]))
    source_part = op(MEAN_SOURCE, f)
    c_out[...] = c
    mean_out[...] = after(source_part[:, :1], source_part[:, 1:] + op(MEAN_STATE, c[:, :-1]))
    message[0] = t[:, RUN - 1]
    message[1] = c[:, RUN - 1]


def join_kernel(own, other, init, table, message, kept):
    op = Operators(table)
    later = lax.axis_index("z1") == 1
    mine, theirs = own[0], other[0]
    prefix = jnp.where(later, theirs, 0.0)
    low = jnp.where(later, theirs, mine)
    high = jnp.where(later, mine, theirs)
    message[:4] = op(COARSE + 3, low) + high
    message[4:8] = own[1] + op(LAST_8, prefix)
    message[8] = init[...]
    kept[0] = prefix
    kept[1] = jnp.where(later, other[1], 0.0)


def finish_kernel(c_in, mean_in, kept, own, other, table, out):
    op = Operators(table)
    at = place()
    second = at >= 2
    at_start = at % 2 == 0
    mine, theirs, theirs_c = own[:4], other[:4], other[4:8]
    init = own[8] + other[8]
    low = jnp.where(second, theirs, mine)
    high = jnp.where(second, mine, theirs)
    total = op(COARSE + 4, low) + high
    state = [init]
    for x in range(3):
        state.append(op(COARSE + 5, state[x]) + total[x])
    state = jnp.stack(state)
    part = jnp.where(second, low, 0.0)
    part_c = jnp.where(second, theirs_c, 0.0)
    carry = kept[0] + jnp.where(at_start, part, op(COARSE + 3, part))
    before = kept[1] + jnp.where(at_start, part_c, op(LAST_8, part))
    by_8, by_16 = op(COARSE + 3, state), op(COARSE + 4, state)
    by_24 = op(COARSE + 3, by_16)
    carry = carry + jnp.where(
        at == 0, state, jnp.where(at == 1, by_8, jnp.where(at == 2, by_16, by_24))
    )
    to_last = jnp.where(at == 1, state, jnp.where(at == 2, by_8, by_16))
    before = before + op(LAST_8, to_last)
    ends = theirs_c[:3] + op(LAST_16, low[:3]) + op(LAST_32, state[:3])
    before = jnp.where(at == 0, jnp.concatenate([init[None], ends], axis=0), before)
    spread = carry[:, None]
    for level in range(3):
        spread = after(spread, op(COARSE + level, spread))
    added = op(DEFECT, spread)
    shift = after(before[:, None], added[:, :-1])
    c = c_in[...] + added
    mean = mean_in[...] + op(MEAN_STATE, shift)
    out[:, :8] = c.reshape(GROUP, 8, COLS)
    out[:, 8:] = mean.reshape(GROUP, 8, COLS)


def backward_kernel(got, rows_t, col, out, own_out):
    odd, lower = parity() == 1, lax.axis_index("sp") == 1
    got_v = got[...]
    parts = [got_v[:, :8], got_v[:, 8:]]
    shape = parts[0].shape
    sub = iota(shape, 1)
    origin = jnp.logical_and(iota(shape, 0) == 0, jnp.logical_and(sub == 0, iota(shape, 2) == 0))
    origin = jnp.logical_and(origin, jnp.logical_not(odd))
    constants = [jnp.where(odd, 0.0, v[0, :1, :1] * (1.0 / (ROWS * COLS))) for v in parts]
    parts = [jnp.where(origin, 0.0, v) for v in parts]
    flat = lambda v: v.reshape(HALF, COLS)
    left = [flat(jnp.where(sub < QUAD, v, -v)) for v in parts]
    right = [flat(flip(v)) for v in parts]
    product = table_times(rows_t[...], jnp.concatenate(left + right, axis=1), THREE)
    sign = alternating((HALF, COLS))
    lane = iota((HALF, COLS), 1)
    own_sign = jnp.where(jnp.logical_and(odd, lower), -1.0, 1.0)
    sent_sign = jnp.where(jnp.logical_and(odd, jnp.logical_not(lower)), -1.0, 1.0)
    zero_mode = jnp.where(odd, 0.0, 0.5)
    for n, v in enumerate(parts):
        e = product[:, COLS * n : COLS * (n + 1)]
        f = product[:, COLS * (n + 2) : COLS * (n + 3)]
        y = jnp.where(lane < LANES, e + sign * swap(e), swap(f) + sign * f)
        first_u, first_v = v[0, :1], v[0, QUAD : QUAD + 1]
        edge = e + zero_mode * (sign * first_v - first_u)
        y = jnp.where(lane % LANES == 0, edge, y)
        part = times_table(y, col[...], THREE) + constants[n]
        out[n] = sent_sign * part
        own_out[n] = own_sign * part


PARAMS = pltpu.CompilerParams(vmem_limit_bytes=32 * 1024 * 1024)


def call(kernel, shapes, args, hbm=False, scratch=()):
    space = pltpu.HBM if hbm else pltpu.VMEM
    return pl.pallas_call(
        kernel,
        out_shape=[
            jax.ShapeDtypeStruct(s, jnp.float32) if isinstance(s, tuple) else s for s in shapes
        ],
        in_specs=[pl.BlockSpec(memory_space=space)] * len(args),
        out_specs=[pl.BlockSpec(memory_space=pltpu.VMEM)] * len(shapes),
        scratch_shapes=scratch,
        compiler_params=PARAMS,
    )(*args)


def shards(initial, source):
    rows = row_table()
    forward, backward = column_tables()
    forward, backward = joined_table(forward, SIX), joined_table(backward, THREE)
    rows_split = split_table(rows, 3)
    rows_t_split = split_table(rows.transpose(0, 2, 1), 2)
    few_rows = rows.reshape(2, GROUP, 8, HALF).astype(np.float32)
    own = source[0]
    swap_two = [(0, 1), (1, 0)]
    src_other = lax.ppermute(own, "sp", swap_two)
    block = (HALF, COLS)
    constants = [rows_split, rows_t_split, few_rows, mode_table()]
    args = [own, initial, *(jnp.asarray(a) for a in constants)]
    bf16 = jnp.bfloat16
    src, init, rows_v, rows_t_v, few, table = call(
        prepare_kernel,
        [
            block,
            block,
            jax.ShapeDtypeStruct((HALF, 3 * HALF), bf16),
            jax.ShapeDtypeStruct((HALF, 2 * HALF), bf16),
            (8, HALF),
            (16 * N_OPS, COLS),
        ],
        [pltpu.with_memory_space_constraint(a, pltpu.HBM) for a in args],
        hbm=True,
        scratch=[pltpu.SemaphoreType.DMA((6,))],
    )
    (sent,) = call(forward_kernel, [block], [src, src_other, forward, rows_v])
    got = lax.all_to_all(sent.reshape(GROUP, 8, COLS), PLANE, 0, 0, tiled=True)
    runs, ends = (4, RUN, 8, COLS), (2, 4, 8, COLS)
    c, mean, message = call(scan_kernel, [runs, runs, ends], [got, table])
    init, message = lax.optimization_barrier((init, message))
    other = lax.ppermute(message, ("z1", "sp"), [(i, i ^ 3) for i in range(4)])
    (init_part,) = call(initial_kernel, [(8, COLS)], [init, forward, few])
    message, kept = call(
        join_kernel, [(9, 8, COLS), ends], [message, other, init_part, table]
    )
    other = lax.ppermute(message, ("zh", "z1", "sp"), [(i, i ^ 7) for i in range(8)])
    (back,) = call(
        finish_kernel,
        [(GROUP, 16, COLS)],
        [c, mean, kept, message, other, table],
    )
    modes = lax.all_to_all(back, PLANE, 0, 0, tiled=True)
    part, own_part = call(
        backward_kernel, [(2, HALF, COLS), (2, HALF, COLS)], [modes, rows_t_v, backward]
    )
    other_part = lax.ppermute(part, "sp", swap_two)
    return own_part[:1] + other_part[:1], own_part[1:] + other_part[1:]


def solution(mesh):
    mesh = jax.sharding.Mesh(mesh.devices.reshape(MESH_SHAPE), MESH_AXES)
    by_block = P(MESH_AXES[:-1], "sp", None)
    return jax.shard_map(
        shards,
        mesh=mesh,
        in_specs=(P("sp", None), by_block),
        out_specs=(by_block, by_block),
        check_vma=False,
    )
```
